1024 devices in a mesh: dp: 128 (over x, z, core), fsdp: 8 (over y).
Axes of the slice: x: 8, y: 8, z: 8, core: 2. Of those that a mesh axis runs over, the one named last changes fastest.
Arguments:
- frames: bfloat16 [262144, 1024], P(('dp', 'fsdp')), may hold values from -6 to 6
- lengths: int32 [1024], replicated, may hold values from 1 to 768, 262144 in all
- taps: bfloat16 [31, 1024], P(None, 'fsdp'), may hold values from -1.8 to 1.8
- conv_bias: bfloat16 [1024], P('fsdp'), may hold values from -3 to 3
- norm_gain: bfloat16 [1024], P('fsdp'), may hold values from 0.5 to 2
- proj_weight: bfloat16 [1024, 1024], P(None, 'fsdp'), may hold values from -0.1875 to 0.1875
- cotangent: bfloat16 [262144, 1024], P(('dp', 'fsdp')), may hold values from -6 to 6
Outputs:
- outputs: bfloat16 [262144, 1024], P(('dp', 'fsdp'))
- frame_grad: bfloat16 [262144, 1024], P(('dp', 'fsdp'))
- proj_grad: float32 [1024, 1024], P('dp', 'fsdp')
The draws below stay inside these ranges and needn't reach their ends.
Inputs may be any that keep to these rules, and one draw needn't show every extreme that they name: The lengths sum to 262144; the longest recording has exactly 768 frames.
All inputs are finite; a program needn't handle non-finite values.
Results may differ from the reference program's by a relative error of at most 0.0049.
Values may be sent and summed in bfloat16 or wider, within the bound.
A program may use at most 32 MiB of HBM per device.

```python
import math
import jax
import jax.numpy as jnp
import numpy as np
from jax import lax

D = 1024
TAPS = 31
TOK_DEV = 256
MEAN_LEN = 256
FRAMES = 262144
RECS = 1024


def draw_taps(key, part):
    key = jax.random.fold_in(key, 11)
    first, second = jax.random.split(key)
    channel_scale = jnp.exp(jax.random.uniform(second, (1, D), jnp.float32, math.log(0.3), math.log(3.0)))
    base = jnp.clip(jax.random.normal(first, (TAPS, D), jnp.float32), -3.0, 3.0)
    return (0.2 * base * channel_scale).astype(jnp.bfloat16)


def level_of(own_key, extent, pieces, low, top_value):
    def one(axis_at, shards_of):
        heights = jax.random.uniform(jax.random.fold_in(jax.random.fold_in(own_key, 6), axis_at), (shards_of,), jnp.float32, low / len(pieces), top_value / len(pieces))
        return jnp.repeat(jnp.exp(heights), extent[axis_at] // shards_of).reshape((-1,) + (1,) * (len(extent) - axis_at - 1))

    level = one(*pieces[0])
    for cut in pieces[1:]:
        level = level * one(*cut)
    return level


def split_up(amount, total, reach, slope):
    weights = [(1 << 20) // math.isqrt(grade ** slope) + 1 for grade in range(2, amount + 1)]
    surplus, given = total - reach - (amount - 1), [1] * (amount - 1)
    while surplus > 0:
        candidates = [i for i in range(amount - 1) if given[i] < reach]
        mass, budget = sum([weights[i] for i in candidates]), surplus
        for i in candidates:
            more = min(reach - given[i], max(1, budget * weights[i] // mass), surplus)
            given[i] = given[i] + more
            surplus = surplus - more
    return np.array([reach] + given)


def uneven(own_key, amount, total, bound, lean):
    if amount == 2:
        one = jax.random.randint(own_key, (), max(1, total - bound), min(bound, total - 1) + 1)
        return jnp.stack([one, total - one])
    tallies = jnp.asarray(split_up(amount, total, bound, lean), jnp.int32)
    couples = (amount - 1) // 2
    giver, sink = tallies[1:1 + 2 * couples:2], tallies[2:2 + 2 * couples:2]
    room = jnp.minimum(giver - 1, bound - sink)
    moved = jax.random.randint(jax.random.fold_in(own_key, 1), (couples,), 0, 1 << 20) % (room + 1)
    tallies = tallies.at[1:1 + 2 * couples:2].set(giver - moved).at[2:2 + 2 * couples:2].set(sink + moved)
    return tallies[jax.random.permutation(jax.random.fold_in(own_key, 2), amount)]


def normal_values(rng, extent, width, limit, pieces=(), kind=jnp.bfloat16):
    values = jax.random.normal(rng, extent, jnp.float32) * width
    if len(pieces) > 0:
        values = level_of(rng, extent, pieces, -0.22, 0.18) * values
    return jnp.clip(values, min=-limit, max=limit).astype(kind)


def setup_inputs(seed: int = 0) -> dict:
    arg_keys = jax.random.split(jax.random.key(seed), 8)
    return {
        "frames": normal_values(arg_keys[0], (FRAMES, D), 1.0, 6.0, ((0, 1024),)),
        "lengths": uneven(arg_keys[1], RECS, FRAMES, 3 * MEAN_LEN, 2).astype(jnp.int32),
        "taps": draw_taps(jax.random.fold_in(arg_keys[7], 71), 0),
        "conv_bias": normal_values(arg_keys[3], (D,), 0.5, 3.0, ((0, 8),)),
        "norm_gain": jnp.clip(jnp.exp(math.log(2.0) - 1.3862944 * jax.random.uniform(arg_keys[4], (D,), jnp.float32) ** level_of(arg_keys[4], (D,), ((0, 8),), -0.2, 0.2)), 0.5, 2.0).astype(jnp.bfloat16),
        "proj_weight": normal_values(arg_keys[5], (D, D), D ** -0.5, 0.1875, ((1, 8),)),
        "cotangent": normal_values(arg_keys[6], (FRAMES, D), 1.0, 6.0, ((0, 1024),)),
    }


def locate(global_rows, lengths):
    ends = jnp.cumsum(lengths).astype(jnp.int32)
    starts = (ends - lengths).astype(jnp.int32)
    record = lax.optimization_barrier(jnp.sum((ends[None, :] <= global_rows[:, None]).astype(jnp.int32), axis=1)).astype(jnp.int32)
    chosen = jnp.arange(lengths.shape[0], dtype=jnp.int32)[None, :] == record[:, None]
    start = lax.optimization_barrier(jnp.sum(jnp.where(chosen, starts[None, :], 0), axis=1)).astype(jnp.int32)
    span = lax.optimization_barrier(jnp.sum(jnp.where(chosen, lengths[None, :], 0), axis=1)).astype(jnp.int32)
    return ((global_rows - start).astype(jnp.int32), span)

def depthwise(window, taps, bias, offsets, span):
    margin = (taps.shape[0] - 1) // 2
    row_count = window.shape[0] - 2 * margin
    result = jnp.zeros((row_count, window.shape[1]), jnp.float32) + bias
    for tap in range(taps.shape[0]):
        moved = offsets + (tap - margin)
        valid = ((moved >= 0) & (moved < span)).astype(jnp.float32)[:, None]
        result = result + taps[tap] * window[tap:tap + row_count] * valid
    return result

def depthwise_back(grads, taps, offsets, span):
    margin = (taps.shape[0] - 1) // 2
    row_count = grads.shape[0] - 2 * margin
    result = jnp.zeros((row_count, grads.shape[1]), jnp.float32)
    for tap in range(taps.shape[0]):
        start = 2 * margin - tap
        moved = offsets + (margin - tap)
        valid = ((moved >= 0) & (moved < span)).astype(jnp.float32)[:, None]
        result = result + taps[tap] * grads[start:start + row_count] * valid
    return result

def forward(window, offsets, span, taps_float, bias_float, gain_float):
    conv_out = depthwise(window.astype(jnp.float32), taps_float, bias_float, offsets, span)
    centre = conv_out - lax.optimization_barrier(jnp.mean(conv_out, axis=-1, keepdims=True))
    inverse = lax.rsqrt(lax.optimization_barrier(jnp.mean(centre * centre, axis=-1, keepdims=True)) + 1e-05)
    normed = centre * inverse
    scaled = normed * gain_float
    sigmoid_gate = jax.nn.sigmoid(scaled)
    swished = (scaled * sigmoid_gate).astype(jnp.bfloat16)
    return (normed, inverse, scaled, sigmoid_gate, swished)

def backward(grad_out, state, weight, gain_float):
    normed, inverse, scaled, sigmoid_gate, swished = state
    grad_swish = lax.dot_general(grad_out, weight, (((1,), (1,)), ((), ())), preferred_element_type=jnp.float32)
    grad_scaled = grad_swish * (sigmoid_gate + scaled * sigmoid_gate * (1.0 - sigmoid_gate))
    grad_normed = grad_scaled * gain_float
    return inverse * (grad_normed - lax.optimization_barrier(jnp.mean(grad_normed, axis=-1, keepdims=True)) - normed * lax.optimization_barrier(jnp.mean(grad_normed * normed, axis=-1, keepdims=True)))

def reference(frames, lengths, taps, conv_bias, norm_gain, proj_weight, cotangent):
    margin = (TAPS - 1) // 2
    blocks = FRAMES // TOK_DEV
    lengths_int = lengths.astype(jnp.int32)
    stacked = jnp.pad(jnp.stack([frames, cotangent]), ((0, 0), (2 * margin, 2 * margin), (0, 0)))
    taps_float = taps.astype(jnp.float32)
    bias_float = conv_bias.astype(jnp.float32)
    gain_float = norm_gain.astype(jnp.float32)

    def advance(total, index):
        first_row = (index * TOK_DEV).astype(jnp.int32)
        wide = lax.dynamic_slice_in_dim(stacked, first_row, TOK_DEV + 4 * margin, 1)
        rows = first_row - margin + jnp.arange(TOK_DEV + 2 * margin, dtype=jnp.int32)
        offsets, span = locate(rows, lengths_int)
        state = forward(wide[0], offsets, span, taps_float, bias_float, gain_float)
        swished_mid = state[4][margin:margin + TOK_DEV]
        grad_window = backward(wide[1][margin:margin + TOK_DEV + 2 * margin], state, proj_weight, gain_float)
        outputs = jnp.dot(swished_mid, proj_weight, preferred_element_type=jnp.float32).astype(jnp.bfloat16)
        grad_values = depthwise_back(grad_window, taps_float, offsets[margin:margin + TOK_DEV], span[margin:margin + TOK_DEV])
        frame_grad = grad_values.astype(jnp.bfloat16)
        cot_mid = wide[1][2 * margin:2 * margin + TOK_DEV]
        weight_term = lax.dot_general(swished_mid, cot_mid, (((0,), (0,)), ((), ())), preferred_element_type=jnp.float32)
        return (total + weight_term, (outputs, frame_grad))
    total, (outputs, frame_grad) = lax.scan(advance, jnp.zeros((D, D), jnp.float32), jnp.arange(blocks, dtype=jnp.int32))
    return (outputs.reshape(FRAMES, D), frame_grad.reshape(FRAMES, D), total * (1.0 / RECS))
```

```python
import jax
import jax.numpy as jnp
from jax import lax
from jax.experimental import pallas as pl
from jax.experimental.pallas import tpu as pltpu
from jax.sharding import PartitionSpec as P

MESH = pl.DeviceIdType.MESH
F32 = jnp.float32
BF16 = jnp.bfloat16
N = 8
LANES = 128
ROWS = 256
D = 1024
TAPS = 31
HALO = 16
WIN = ROWS + 2 * HALO
GROUP = 64


def fused(frames, lengths, taps, bias, gain, weight, cot,
          out, fgrad, pgrad,
          pack, gpack, pack_f, tap_all, gain_all, tap_f, gain_f,
          halo, fwin, gwin, off_b, rem_b,
          conv, normed, dfac, inv_b, sum_a, sum_b,
          swished, swt, swt_f, swt_rx, cot_sib, w_all,
          tx1, rx1, acc2, tx2, rx2, tx3, rx3,
          tap_s, tap_r, gain_s, gain_r, halo_s, halo_r, ghalo_s, ghalo_r,
          cot_s, cot_r, swt_s, swt_r, wr_s, wr_r, wl_s, wl_r, ws_s, ws_r,
          r1_s, r1_r, r2_s, r2_r, r3_s, r3_r, loc_s):
    dp = lax.axis_index("dp")
    y = lax.axis_index("fsdp")
    core = dp % 2
    z = (dp // 2) % N
    x = dp // (2 * N)
    a = x * (1 - core) + z * core
    b = z * (1 - core) + x * core

    def chip(a_to, b_to):
        return (a_to * (N - (N - 1) * core) + b_to * (1 + (N - 1) * core)) * 2 + core

    def y_peer(k):
        return (dp, (y + k) % N)

    def a_peer(k):
        return (chip((a + k) % N, b), y)

    def b_peer(k):
        return (chip(a, (b + k) % N), y)

    sibling = (dp + 1 - 2 * core, y)
    place = dp * N + y
    count = 128 * N
    after = (place + 1) % count
    before = (place + count - 1) % count
    next_dev = (after // N, after % N)
    prev_dev = (before // N, before % N)

    def remote(src, dst, send, recv, to):
        return pltpu.make_async_remote_copy(
            src_ref=src, dst_ref=dst, send_sem=send, recv_sem=recv,
            device_id=to, device_id_type=MESH)

    barrier = pltpu.get_barrier_semaphore()
    peers = [sibling, next_dev, prev_dev]
    for k in range(1, N):
        peers += [y_peer(k), a_peer(k), b_peer(k)]
    for peer in peers:
        pl.semaphore_signal(barrier, inc=1, device_id=peer, device_id_type=MESH)

    pack_f[0:TAPS, :] = taps[...].astype(F32)
    pack_f[TAPS:TAPS + 1, :] = bias[...].astype(F32)
    pack[...] = pack_f[...].astype(BF16)
    gpack[...] = jnp.broadcast_to(gain[...].astype(F32), (16, LANES)).astype(BF16)

    ends = lengths[...].astype(F32)
    lane = lax.broadcasted_iota(jnp.int32, (N, LANES), 1)
    row8 = lax.broadcasted_iota(jnp.int32, (N, LANES), 0)
    step = 1
    while step < LANES:
        ends = ends + jnp.where(lane >= step, pltpu.roll(ends, step, 1), 0.0)
        step *= 2
    total = jnp.broadcast_to(jnp.max(ends, axis=1, keepdims=True), (N, LANES))
    before_sum = jnp.where(row8 >= 1, pltpu.roll(total, 1, 0), 0.0)
    step = 1
    while step < N:
        before_sum = before_sum + jnp.where(row8 >= step, pltpu.roll(before_sum, step, 0), 0.0)
        step *= 2
    ends = ends + before_sum - (place * ROWS).astype(F32)
    acc2[0, 0] = ends

    def locate(group, carry):
        base = pl.multiple_of(group * GROUP, GROUP)
        rows = (lax.broadcasted_iota(jnp.int32, (GROUP, LANES), 0) + base).astype(F32)
        start = jnp.full((GROUP, LANES), -1e9, F32)
        stop = jnp.full((GROUP, LANES), 1e9, F32)
        for i in range(N):
            edge = jnp.broadcast_to(acc2[0, 0, i:i + 1, :], (GROUP, LANES))
            passed = edge <= rows
            start = jnp.maximum(start, jnp.where(passed, edge, -1e9))
            stop = jnp.minimum(stop, jnp.where(passed, 1e9, edge))
        first = (-(place * ROWS)).astype(F32)
        start = jnp.maximum(jnp.max(start, axis=1, keepdims=True), first)
        stop = jnp.min(stop, axis=1, keepdims=True)
        off_b[pl.ds(base, GROUP), :] = rows - start
        rem_b[pl.ds(base, GROUP), :] = stop - rows
        return carry

    lax.fori_loop(0, ROWS // GROUP, locate, 0)

    for c in range(N):
        fwin[c, HALO:HALO + ROWS, :] = frames[:, c * LANES:(c + 1) * LANES].astype(F32)

    pl.semaphore_wait(barrier, len(peers))

    order = (4, 3, 5, 2, 6, 1, 7)
    tap_copies = {}
    gain_copies = {}
    for k in order:
        tap_copies[k] = remote(pack, tap_all.at[y], tap_s.at[k - 1], tap_r.at[k - 1], y_peer(k))
        tap_copies[k].start()
    halo_down = remote(frames.at[ROWS - HALO:ROWS], halo.at[0], halo_s.at[0], halo_r.at[0], next_dev)
    halo_up = remote(frames.at[0:HALO], halo.at[1], halo_s.at[1], halo_r.at[1], prev_dev)
    halo_down.start()
    halo_up.start()
    for k in order:
        gain_copies[k] = remote(gpack, gain_all.at[y], gain_s.at[k - 1], gain_r.at[k - 1], y_peer(k))
        gain_copies[k].start()

    half = D // 2
    my_half = pl.ds(pl.multiple_of(core * half, half), half)
    other_half = pl.ds(pl.multiple_of((1 - core) * half, half), half)

    def shard(owner):
        return pl.ds(pl.multiple_of(owner * LANES, LANES), LANES)

    def w_block(owner, rows):
        return w_all.at[rows, shard(owner)]

    right, left = y_peer(1), y_peer(N - 1)
    w_right, w_left, w_side = {}, {}, {}

    def send_right(s):
        owner = (y - (s - 1) + N) % N
        src = weight.at[my_half, :] if s == 1 else w_block(owner, my_half)
        w_right[s] = remote(src, w_block(owner, my_half), wr_s.at[s - 1], wr_r.at[s - 1], right)
        w_right[s].start()

    def send_left(s):
        owner = (y + (s - 1)) % N
        src = weight.at[my_half, :] if s == 1 else w_block(owner, my_half)
        w_left[s] = remote(src, w_block(owner, my_half), wl_s.at[s - 1], wl_r.at[s - 1], left)
        w_left[s].start()

    def send_side(slot, owner):
        w_side[slot] = remote(w_block(owner, my_half), w_block(owner, my_half),
                              ws_s.at[slot], ws_r.at[slot], sibling)
        w_side[slot].start()

    def w_service(s):
        if s <= 4:
            owner = (y - s + N) % N
            remote(w_block(owner, my_half), w_block(owner, my_half),
                   wr_s.at[s - 1], wr_r.at[s - 1], right).wait_recv()
            if s < 4:
                send_right(s + 1)
        if s <= 3:
            owner_l = (y + s) % N
            remote(w_block(owner_l, my_half), w_block(owner_l, my_half),
                   wl_s.at[s - 1], wl_r.at[s - 1], left).wait_recv()
            if s < 3:
                send_left(s + 1)
        if s <= 4:
            send_side(s - 1, (y - s + N) % N)
        if s <= 3:
            send_side(4 + s - 1, (y + s) % N)

    send_right(1)
    send_left(1)
    cot_copy = remote(cot, cot_sib, cot_s, cot_r, sibling)
    cot_copy.start()
    own_w = pltpu.make_async_copy(weight, w_all.at[:, shard(y)], loc_s)
    own_w.start()

    tap_f[y] = pack[...].astype(F32)
    for k in range(1, N):
        source = (y - k + N) % N
        remote(tap_all.at[source], tap_all.at[source], tap_s.at[k - 1], tap_r.at[k - 1],
               y_peer(N - k)).wait_recv()
        tap_f[source] = tap_all[source].astype(F32)
    halo_down.wait_recv()
    halo_up.wait_recv()
    for c in range(N):
        fwin[c, 0:HALO, :] = halo[0, :, c * LANES:(c + 1) * LANES].astype(F32)
        fwin[c, HALO + ROWS:WIN, :] = halo[1, :, c * LANES:(c + 1) * LANES].astype(F32)

    def convolve(window, pair, base, reverse):
        off = off_b[pl.ds(base, GROUP), :]
        rem = rem_b[pl.ds(base, GROUP), :]
        sums = []
        for c in pair:
            if reverse:
                sums.append(jnp.zeros((GROUP, LANES), F32))
            else:
                sums.append(jnp.broadcast_to(tap_f[c, TAPS:TAPS + 1, :], (GROUP, LANES)))
        for j in range(TAPS):
            d = j - (TAPS - 1) // 2
            together = off >= float(-d) if d < 0 else rem > float(d)
            tap = TAPS - 1 - j if reverse else j
            for i, c in enumerate(pair):
                value = window[c, pl.ds(base + (j + 1), GROUP), :]
                if d != 0:
                    value = jnp.where(together, value, 0.0)
                sums[i] = sums[i] + tap_f[c, tap:tap + 1, :] * value
        return sums

    def forward_pair(p):
        def body(group, carry):
            base = pl.multiple_of(group * GROUP, GROUP)
            one, two = convolve(fwin, (2 * p, 2 * p + 1), base, False)
            conv[2 * p, pl.ds(base, GROUP), :] = one
            conv[2 * p + 1, pl.ds(base, GROUP), :] = two
            return carry

        lax.fori_loop(0, ROWS // GROUP, body, 0)

    for p in range(4):
        forward_pair(p)
        if p == 2:
            w_service(1)

    def over_features(make):
        def body(group, carry):
            base = pl.multiple_of(group * GROUP, GROUP)
            rows = pl.ds(base, GROUP)
            sum_a[rows, :] = make(rows)
            return carry

        lax.fori_loop(0, ROWS // GROUP, body, 0)
        return jnp.sum(sum_a[...], axis=1, keepdims=True) * (1.0 / D)

    def plain(rows):
        total = conv[0, rows, :]
        for c in range(1, N):
            total = total + conv[c, rows, :]
        return total

    sum_b[...] = jnp.broadcast_to(over_features(plain), (ROWS, LANES))

    def squares(rows):
        mean = sum_b[rows, :]
        total = jnp.zeros((GROUP, LANES), F32)
        for c in range(N):
            centre = conv[c, rows, :] - mean
            total = total + centre * centre
        return total

    inv_b[...] = jnp.broadcast_to(lax.rsqrt(over_features(squares) + 1e-05), (ROWS, LANES))

    gain_f[y] = gpack[...].astype(F32)
    for k in range(1, N):
        source = (y - k + N) % N
        remote(gain_all.at[source], gain_all.at[source], gain_s.at[k - 1], gain_r.at[k - 1],
               y_peer(N - k)).wait_recv()
        gain_f[source] = gain_all[source].astype(F32)

    def swish_block(c, carry):
        gain_row = gain_f[c, 0:1, :]
        for h in range(2):
            rows = pl.ds(h * 128, 128)
            unit = (conv[c, rows, :] - sum_b[rows, :]) * inv_b[rows, :]
            normed[c, rows, :] = unit
            scaled = unit * gain_row
            gate = 1.0 / (1.0 + jnp.exp(-scaled))
            sw = (scaled * gate).astype(BF16)
            dfac[c, rows, :] = (gate + scaled * gate * (1.0 - gate)) * gain_row
            swished[rows, shard(c)] = sw
            turned = jnp.transpose(sw.astype(F32)).reshape(N, 2, 8, 128)
            swt[0, c, :, h * 128:(h + 1) * 128] = turned[:, 0].reshape(64, 128).astype(BF16)
            swt_f[:, c, :, h * 128:(h + 1) * 128] = turned[:, 1]
        return carry

    lax.fori_loop(0, N, swish_block, 0)
    for i in range(N):
        swt[1, i] = swt_f[i].reshape(64, ROWS).astype(BF16)

    swt_copy = remote(swt.at[1 - core], swt_rx, swt_s, swt_r, sibling)
    swt_copy.start()
    w_service(2)
    cot_copy.wait_recv()
    swt_copy.wait_recv()

    for n in range(4):
        cols = slice(n * 256, (n + 1) * 256)
        part = jnp.dot(swt[core].reshape(512, ROWS), cot[:, cols], preferred_element_type=F32)
        part = part + jnp.dot(swt_rx[...].reshape(512, ROWS), cot_sib[:, cols], preferred_element_type=F32)
        tx1[:, :, cols] = part.astype(BF16).reshape(N, 64, 256)

    r1 = {}
    for k in order:
        r1[k] = remote(tx1.at[(a + k) % N], rx1.at[k - 1], r1_s.at[k - 1], r1_r.at[k - 1], a_peer(k))
        r1[k].start()

    w_service(3)
    w_service(4)
    own_w.wait()
    for s in range(1, 5):
        owner = (y - s + N) % N
        remote(w_block(owner, other_half), w_block(owner, other_half),
               ws_s.at[s - 1], ws_r.at[s - 1], sibling).wait_recv()
    for s in range(1, 4):
        owner = (y + s) % N
        remote(w_block(owner, other_half), w_block(owner, other_half),
               ws_s.at[4 + s - 1], ws_r.at[4 + s - 1], sibling).wait_recv()

    sum_a[...] = jnp.zeros((ROWS, LANES), F32)
    sum_b[...] = jnp.zeros((ROWS, LANES), F32)
    for n in range(4):
        grad = lax.dot_general(cot[...], w_all[n * 256:(n + 1) * 256, :], (((1,), (1,)), ((), ())),
                               preferred_element_type=F32)
        for i in range(2):
            c = 2 * n + i
            grad_normed = grad[:, i * LANES:(i + 1) * LANES] * dfac[c]
            gwin[c, HALO:HALO + ROWS, :] = grad_normed
            sum_a[...] += grad_normed
            sum_b[...] += grad_normed * normed[c]
    sum_a[...] = jnp.broadcast_to(jnp.sum(sum_a[...], axis=1, keepdims=True) * (1.0 / D), (ROWS, LANES))
    sum_b[...] = jnp.broadcast_to(jnp.sum(sum_b[...], axis=1, keepdims=True) * (1.0 / D), (ROWS, LANES))

    def norm_back(c, carry):
        gwin[c, HALO:HALO + ROWS, :] = inv_b[...] * (
            gwin[c, HALO:HALO + ROWS, :] - sum_a[...] - normed[c] * sum_b[...])
        return carry

    lax.fori_loop(0, N, norm_back, 0)

    ghalo_down = remote(gwin.at[:, ROWS:ROWS + HALO, :], gwin.at[:, 0:HALO, :],
                        ghalo_s.at[0], ghalo_r.at[0], next_dev)
    ghalo_up = remote(gwin.at[:, HALO:2 * HALO, :], gwin.at[:, ROWS + HALO:WIN, :],
                      ghalo_s.at[1], ghalo_r.at[1], prev_dev)
    ghalo_down.start()
    ghalo_up.start()

    for n in range(4):
        cols = slice(n * 256, (n + 1) * 256)
        out[:, cols] = jnp.dot(swished[...], w_all[:, cols], preferred_element_type=F32).astype(BF16)

    ghalo_down.wait_recv()
    ghalo_up.wait_recv()

    def backward_pair(p):
        def body(group, carry):
            base = pl.multiple_of(group * GROUP, GROUP)
            pair = convolve(gwin, (2 * p, 2 * p + 1), base, True)
            for i in range(2):
                c = 2 * p + i
                fgrad[pl.ds(base, GROUP), c * LANES:(c + 1) * LANES] = pair[i].astype(BF16)
            return carry

        lax.fori_loop(0, ROWS // GROUP, body, 0)

    def reduce_a():
        for k in range(1, N):
            remote(tx1.at[0], rx1.at[k - 1], r1_s.at[k - 1], r1_r.at[k - 1], a_peer(N - k)).wait_recv()
        for c in range(N):
            cols = slice(c * LANES, (c + 1) * LANES)
            total = tx1[a, :, cols].astype(F32)
            for k in range(1, N):
                total = total + rx1[k - 1, :, cols].astype(F32)
            acc2[:, c] = total.reshape(N, 8, LANES)
        for i in range(N):
            tx2[i] = acc2[i].reshape(64, LANES).astype(BF16)
        for k in order:
            remote(tx2.at[(b + k) % N], rx2.at[k - 1], r2_s.at[k - 1], r2_r.at[k - 1], b_peer(k)).start()

    def reduce_b():
        for k in range(1, N):
            remote(tx2.at[0], rx2.at[k - 1], r2_s.at[k - 1], r2_r.at[k - 1], b_peer(N - k)).wait_recv()
        total = acc2[b].reshape(64, LANES)
        for k in range(1, N):
            total = total + rx2[k - 1].astype(F32)
        tx3[...] = total.reshape(N, 8, LANES)
        for k in order:
            remote(tx3.at[(y + k) % N], rx3.at[k - 1], r3_s.at[k - 1], r3_r.at[k - 1], y_peer(k)).start()

    def reduce_y():
        for k in range(1, N):
            remote(tx3.at[0], rx3.at[k - 1], r3_s.at[k - 1], r3_r.at[k - 1], y_peer(N - k)).wait_recv()
        total = tx3[y]
        for k in range(1, N):
            total = total + rx3[k - 1]
        pgrad[...] = total * (1.0 / 1024)

    backward_pair(0)
    backward_pair(1)
    reduce_a()
    backward_pair(2)
    reduce_b()
    backward_pair(3)
    reduce_y()

    for k in range(1, N):
        tap_copies[k].wait_send()
        gain_copies[k].wait_send()
        r1[k].wait_send()
        remote(tx2.at[0], rx2.at[k - 1], r2_s.at[k - 1], r2_r.at[k - 1], b_peer(k)).wait_send()
        remote(tx3.at[0], rx3.at[k - 1], r3_s.at[k - 1], r3_r.at[k - 1], y_peer(k)).wait_send()
    for copy in (halo_down, halo_up, ghalo_down, ghalo_up, cot_copy, swt_copy):
        copy.wait_send()
    for copies in (w_right, w_left, w_side):
        for copy in copies.values():
            copy.wait_send()


def per_device(frames, lengths, taps, conv_bias, norm_gain, proj_weight, cotangent):
    vmem = pl.BlockSpec(memory_space=pltpu.VMEM)
    dma = pltpu.SemaphoreType.DMA
    scratch = [
        pltpu.VMEM((32, LANES), BF16), pltpu.VMEM((16, LANES), BF16), pltpu.VMEM((32, LANES), F32),
        pltpu.VMEM((N, 32, LANES), BF16), pltpu.VMEM((N, 16, LANES), BF16),
        pltpu.VMEM((N, 32, LANES), F32), pltpu.VMEM((N, 16, LANES), F32),
        pltpu.VMEM((2, HALO, D), BF16),
        pltpu.VMEM((N, WIN, LANES), F32), pltpu.VMEM((N, WIN, LANES), F32),
        pltpu.VMEM((ROWS, LANES), F32), pltpu.VMEM((ROWS, LANES), F32),
        pltpu.VMEM((N, ROWS, LANES), F32), pltpu.VMEM((N, ROWS, LANES), F32),
        pltpu.VMEM((N, ROWS, LANES), F32),
        pltpu.VMEM((ROWS, LANES), F32), pltpu.VMEM((ROWS, LANES), F32), pltpu.VMEM((ROWS, LANES), F32),
        pltpu.VMEM((ROWS, D), BF16),
        pltpu.VMEM((2, N, 64, ROWS), BF16), pltpu.VMEM((N, N, 8, ROWS), F32), pltpu.VMEM((N, 64, ROWS), BF16),
        pltpu.VMEM((ROWS, D), BF16), pltpu.VMEM((D, D), BF16),
        pltpu.VMEM((N, 64, D), BF16), pltpu.VMEM((N - 1, 64, D), BF16),
        pltpu.VMEM((N, N, 8, LANES), F32),
        pltpu.VMEM((N, 64, LANES), BF16), pltpu.VMEM((N - 1, 64, LANES), BF16),
        pltpu.VMEM((N, 8, LANES), F32), pltpu.VMEM((N - 1, 8, LANES), F32),
        dma((7,)), dma((7,)), dma((7,)), dma((7,)), dma((2,)), dma((2,)), dma((2,)), dma((2,)),
        dma, dma, dma, dma, dma((4,)), dma((4,)), dma((3,)), dma((3,)), dma((7,)), dma((7,)),
        dma((7,)), dma((7,)), dma((7,)), dma((7,)), dma((7,)), dma((7,)), dma,
    ]
    return pl.pallas_call(
        fused,
        out_shape=(
            jax.ShapeDtypeStruct((ROWS, D), BF16),
            jax.ShapeDtypeStruct((ROWS, D), BF16),
            jax.ShapeDtypeStruct((8, LANES), F32),
        ),
        in_specs=[vmem] * 7,
        out_specs=(vmem, vmem, vmem),
        scratch_shapes=scratch,
        compiler_params=pltpu.CompilerParams(
            collective_id=0, has_side_effects=True, vmem_limit_bytes=40 * 1024 * 1024),
        name="fused_module",
    )(frames, lengths.reshape(N, LANES), taps, conv_bias.reshape(1, LANES),
      norm_gain.reshape(1, LANES), proj_weight, cotangent)


def solution(mesh):
    rows = P(("dp", "fsdp"), None)
    in_specs = (rows, P(), P(None, "fsdp"), P("fsdp"), P("fsdp"), P(None, "fsdp"), rows)
    out_specs = (rows, rows, P("dp", "fsdp"))
    return jax.shard_map(
        per_device, mesh=mesh, in_specs=in_specs, out_specs=out_specs, check_vma=False)
```

```python
import jax
import jax.numpy as jnp
from jax import lax
from jax.experimental import pallas as pl
from jax.experimental.pallas import tpu as pltpu
from jax.sharding import PartitionSpec as P

MESH = pl.DeviceIdType.MESH
F32 = jnp.float32
BF16 = jnp.bfloat16
N = 8
LANES = 128
ROWS = 256
D = 1024
TAPS = 31
HALO = 16
WIN = ROWS + 2 * HALO
GROUP = 64


def fused(frames_h, lengths_h, taps_h, bias_h, gain_h, weight, cot_h,
          out_h, fgrad_h, pgrad_h,
          out, fgrad, pgrad, frames, lengths, taps, bias, gain, cot,
          pack, gpack, pack_f, tap_all, gain_all, tap_f, gain_f,
          halo, fwin, gwin, off_b, rem_b,
          conv, normed, dfac, inv_b, sum_a, sum_b,
          swished, swt, swt_f, swt_rx, cot_sib, w_all,
          tx1, rx1, acc2, tx2, rx2, tx3, rx3,
          tap_s, tap_r, gain_s, gain_r, halo_s, halo_r, ghalo_s, ghalo_r,
          cot_s, cot_r, swt_s, swt_r, wr_s, wr_r, wl_s, wl_r, ws_s, ws_r,
          r1_s, r1_r, r2_s, r2_r, r3_s, r3_r, loc_s, done_s):
    dp = lax.axis_index("dp")
    y = lax.axis_index("fsdp")
    core = dp % 2
    z = (dp // 2) % N
    x = dp // (2 * N)
    a = x * (1 - core) + z * core
    b = z * (1 - core) + x * core

    def chip(a_to, b_to):
        return (a_to * (N - (N - 1) * core) + b_to * (1 + (N - 1) * core)) * 2 + core

    def y_peer(k):
        return (dp, (y + k) % N)

    def a_peer(k):
        return (chip((a + k) % N, b), y)

    def b_peer(k):
        return (chip(a, (b + k) % N), y)

    sibling = (dp + 1 - 2 * core, y)
    place = dp * N + y
    count = 128 * N
    after = (place + 1) % count
    before = (place + count - 1) % count
    next_dev = (after // N, after % N)
    prev_dev = (before // N, before % N)

    def remote(src, dst, send, recv, to):
        return pltpu.make_async_remote_copy(
            src_ref=src, dst_ref=dst, send_sem=send, recv_sem=recv,
            device_id=to, device_id_type=MESH)

    loads = [pltpu.make_async_copy(src, dst, loc_s.at[i]) for i, (src, dst) in enumerate((
        (lengths_h, lengths), (taps_h, taps), (bias_h, bias), (gain_h, gain), (frames_h, frames), (cot_h, cot)))]
    for load in loads:
        load.start()

    barrier = pltpu.get_barrier_semaphore()
    order = (4, 3, 5, 2, 6, 1, 7)
    peers = [y_peer(k) for k in order] + [next_dev, prev_dev, sibling]
    for k in order:
        peers += [a_peer(k), b_peer(k)]
    for peer in peers:
        pl.semaphore_signal(barrier, inc=1, device_id=peer, device_id_type=MESH)

    for load in loads[:4]:
        load.wait()

    pack_f[0:TAPS, :] = taps[...].astype(F32)
    pack_f[TAPS:TAPS + 1, :] = bias[...].astype(F32)
    pack[...] = pack_f[...].astype(BF16)
    gpack[...] = jnp.broadcast_to(gain[...].astype(F32), (16, LANES)).astype(BF16)

    pl.semaphore_wait(barrier, len(peers))

    near = (1, 7, 2, 6, 3, 5, 4)
    tap_copies = {}
    gain_copies = {}
    for k in near:
        tap_copies[k] = remote(pack, tap_all.at[y], tap_s.at[k - 1], tap_r.at[k - 1], y_peer(k))
        tap_copies[k].start()
    halo_down = remote(frames_h.at[ROWS - HALO:ROWS], halo.at[0], halo_s.at[0], halo_r.at[0], next_dev)
    halo_up = remote(frames_h.at[0:HALO], halo.at[1], halo_s.at[1], halo_r.at[1], prev_dev)
    halo_down.start()
    halo_up.start()
    half = D // 2
    my_half = pl.ds(pl.multiple_of(core * half, half), half)
    other_half = pl.ds(pl.multiple_of((1 - core) * half, half), half)

    def shard(owner):
        return pl.ds(pl.multiple_of(owner * LANES, LANES), LANES)

    def w_block(owner, rows):
        return w_all.at[rows, shard(owner)]

    right, left = y_peer(1), y_peer(N - 1)
    w_right, w_left, w_side = {}, {}, {}

    quarter = half // 2
    first_part = pl.ds(pl.multiple_of(core * half, quarter), quarter)
    second_part = pl.ds(pl.multiple_of(core * half + quarter, quarter), quarter)

    def send_right(s):
        owner = (y - (s - 1) + N) % N
        rows = first_part if s == 4 else my_half
        src = weight.at[rows, :] if s == 1 else w_block(owner, rows)
        w_right[s] = remote(src, w_block(owner, rows), wr_s.at[s - 1], wr_r.at[s - 1], right)
        w_right[s].start()

    def send_left(s):
        owner = (y + (s - 1)) % N
        rows = second_part if s == 4 else my_half
        src = weight.at[rows, :] if s == 1 else w_block(owner, rows)
        w_left[s] = remote(src, w_block(owner, rows), wl_s.at[s - 1], wl_r.at[s - 1], left)
        w_left[s].start()

    def send_side(slot, owner):
        w_side[slot] = remote(w_block(owner, my_half), w_block(owner, my_half),
                              ws_s.at[slot], ws_r.at[slot], sibling)
        w_side[slot].start()

    def w_service(s):
        below, above = (y - s + N) % N, (y + s) % N
        rows = first_part if s == 4 else my_half
        remote(w_block(below, rows), w_block(below, rows), wr_s.at[s - 1], wr_r.at[s - 1], right).wait_recv()
        if s < 4:
            send_right(s + 1)
            send_side(s - 1, below)
        rows = second_part if s == 4 else my_half
        remote(w_block(above, rows), w_block(above, rows), wl_s.at[s - 1], wl_r.at[s - 1], left).wait_recv()
        if s < 4:
            send_left(s + 1)
            send_side(3 + s, above)
        else:
            send_side(3, below)

    for k in near:
        gain_copies[k] = remote(gpack, gain_all.at[y], gain_s.at[k - 1], gain_r.at[k - 1], y_peer(k))
        gain_copies[k].start()
    send_right(1)
    send_left(1)
    cot_copy = remote(cot_h, cot_sib, cot_s, cot_r, sibling)
    cot_copy.start()
    own_w = pltpu.make_async_copy(weight, w_all.at[:, shard(y)], loc_s.at[6])
    own_w.start()

    ends = lengths[...].astype(F32)
    lane = lax.broadcasted_iota(jnp.int32, (N, LANES), 1)
    row8 = lax.broadcasted_iota(jnp.int32, (N, LANES), 0)
    step = 1
    while step < LANES:
        ends = ends + jnp.where(lane >= step, pltpu.roll(ends, step, 1), 0.0)
        step *= 2
    total = jnp.broadcast_to(jnp.max(ends, axis=1, keepdims=True), (N, LANES))
    before_sum = jnp.where(row8 >= 1, pltpu.roll(total, 1, 0), 0.0)
    step = 1
    while step < N:
        before_sum = before_sum + jnp.where(row8 >= step, pltpu.roll(before_sum, step, 0), 0.0)
        step *= 2
    ends = ends + before_sum - (place * ROWS).astype(F32)
    acc2[0, 0] = ends

    def locate(group, carry):
        base = pl.multiple_of(group * GROUP, GROUP)
        rows = (lax.broadcasted_iota(jnp.int32, (GROUP, LANES), 0) + base).astype(F32)
        start = jnp.full((GROUP, LANES), -1e9, F32)
        stop = jnp.full((GROUP, LANES), 1e9, F32)
        for i in range(N):
            edge = jnp.broadcast_to(acc2[0, 0, i:i + 1, :], (GROUP, LANES))
            passed = edge <= rows
            start = jnp.maximum(start, jnp.where(passed, edge, -1e9))
            stop = jnp.minimum(stop, jnp.where(passed, 1e9, edge))
        first = (-(place * ROWS)).astype(F32)
        start = jnp.maximum(jnp.max(start, axis=1, keepdims=True), first)
        stop = jnp.min(stop, axis=1, keepdims=True)
        off_b[pl.ds(base, GROUP), :] = rows - start
        rem_b[pl.ds(base, GROUP), :] = stop - rows
        return carry

    lax.fori_loop(0, ROWS // GROUP, locate, 0)

    loads[4].wait()
    for c in range(N):
        fwin[c, HALO:HALO + ROWS, :] = frames[:, c * LANES:(c + 1) * LANES].astype(F32)

    def tap_arrives(k):
        source = (y - k + N) % N
        remote(tap_all.at[source], tap_all.at[source], tap_s.at[k - 1], tap_r.at[k - 1],
               y_peer(N - k)).wait_recv()
        tap_f[source] = tap_all[source].astype(F32)
        return source

    def convolve(window, blocks, base, reverse):
        off = off_b[pl.ds(base, GROUP), :]
        rem = rem_b[pl.ds(base, GROUP), :]
        sums = []
        for c in blocks:
            if reverse:
                sums.append(jnp.zeros((GROUP, LANES), F32))
            else:
                sums.append(jnp.broadcast_to(tap_f[c, TAPS:TAPS + 1, :], (GROUP, LANES)))
        for j in range(TAPS):
            d = j - (TAPS - 1) // 2
            together = off >= float(-d) if d < 0 else rem > float(d)
            tap = TAPS - 1 - j if reverse else j
            for i, c in enumerate(blocks):
                value = window[c, pl.ds(base + (j + 1), GROUP), :]
                if d != 0:
                    value = jnp.where(together, value, 0.0)
                sums[i] = sums[i] + tap_f[c, tap:tap + 1, :] * value
        return sums

    def forward_blocks(blocks, first, count, stride):
        def body(group, carry):
            base = pl.multiple_of(first + group * stride, GROUP)
            for c, value in zip(blocks, convolve(fwin, blocks, base, False)):
                conv[c, pl.ds(base, GROUP), :] = value
            return carry

        lax.fori_loop(0, count, body, 0)

    tap_f[y] = pack[...].astype(F32)
    forward_blocks((y,), GROUP, 2, GROUP)
    blocks = (tap_arrives(1), tap_arrives(7))
    forward_blocks(blocks, GROUP, 2, GROUP)
    halo_down.wait_recv()
    halo_up.wait_recv()
    for c in range(N):
        fwin[c, 0:HALO, :] = halo[0, :, c * LANES:(c + 1) * LANES].astype(F32)
        fwin[c, HALO + ROWS:WIN, :] = halo[1, :, c * LANES:(c + 1) * LANES].astype(F32)
    forward_blocks(blocks, 0, 2, ROWS - GROUP)
    forward_blocks((tap_arrives(2), tap_arrives(6)), 0, 4, GROUP)
    w_service(1)
    forward_blocks((tap_arrives(3), tap_arrives(5)), 0, 4, GROUP)
    last = tap_arrives(4)
    forward_blocks((y, last), 0, 2, ROWS - GROUP)
    forward_blocks((last,), GROUP, 2, GROUP)

    def over_features(make):
        def body(group, carry):
            base = pl.multiple_of(group * GROUP, GROUP)
            rows = pl.ds(base, GROUP)
            sum_a[rows, :] = make(rows)
            return carry

        lax.fori_loop(0, ROWS // GROUP, body, 0)
        return jnp.sum(sum_a[...], axis=1, keepdims=True) * (1.0 / D)

    def plain(rows):
        total = conv[0, rows, :]
        for c in range(1, N):
            total = total + conv[c, rows, :]
        return total

    sum_b[...] = jnp.broadcast_to(over_features(plain), (ROWS, LANES))

    def squares(rows):
        mean = sum_b[rows, :]
        total = jnp.zeros((GROUP, LANES), F32)
        for c in range(N):
            centre = conv[c, rows, :] - mean
            total = total + centre * centre
        return total

    inv_b[...] = jnp.broadcast_to(lax.rsqrt(over_features(squares) + 1e-05), (ROWS, LANES))

    gain_f[y] = gpack[...].astype(F32)
    for k in range(1, N):
        source = (y - k + N) % N
        remote(gain_all.at[source], gain_all.at[source], gain_s.at[k - 1], gain_r.at[k - 1],
               y_peer(N - k)).wait_recv()
        gain_f[source] = gain_all[source].astype(F32)

    def swish_block(c, carry):
        gain_row = gain_f[c, 0:1, :]
        for h in range(2):
            rows = pl.ds(h * 128, 128)
            unit = (conv[c, rows, :] - sum_b[rows, :]) * inv_b[rows, :]
            normed[c, rows, :] = unit
            scaled = unit * gain_row
            gate = 1.0 / (1.0 + jnp.exp(-scaled))
            sw = (scaled * gate).astype(BF16)
            dfac[c, rows, :] = (gate + scaled * gate * (1.0 - gate)) * gain_row
            swished[rows, shard(c)] = sw
            turned = jnp.transpose(sw.astype(F32)).reshape(N, 2, 8, 128)
            swt[0, c, :, h * 128:(h + 1) * 128] = turned[:, 0].reshape(64, 128).astype(BF16)
            swt_f[:, c, :, h * 128:(h + 1) * 128] = turned[:, 1]
        return carry

    lax.fori_loop(0, N, swish_block, 0)
    for i in range(N):
        swt[1, i] = swt_f[i].reshape(64, ROWS).astype(BF16)

    swt_copy = remote(swt.at[1 - core], swt_rx, swt_s, swt_r, sibling)
    swt_copy.start()
    loads[5].wait()
    cot_copy.wait_recv()
    swt_copy.wait_recv()

    for n in range(4):
        cols = slice(n * 256, (n + 1) * 256)
        part = jnp.dot(swt[core].reshape(512, ROWS), cot[:, cols], preferred_element_type=F32)
        part = part + jnp.dot(swt_rx[...].reshape(512, ROWS), cot_sib[:, cols], preferred_element_type=F32)
        tx1[:, :, cols] = part.astype(BF16).reshape(N, 64, 256)

    r1 = {}
    for k in order:
        r1[k] = remote(tx1.at[(a + k) % N], rx1.at[k - 1], r1_s.at[k - 1], r1_r.at[k - 1], a_peer(k))
        r1[k].start()

    w_service(2)
    w_service(3)
    w_service(4)
    own_w.wait()
    for s in range(1, 5):
        owner = (y - s + N) % N
        remote(w_block(owner, other_half), w_block(owner, other_half),
               ws_s.at[s - 1], ws_r.at[s - 1], sibling).wait_recv()
    for s in range(1, 4):
        owner = (y + s) % N
        remote(w_block(owner, other_half), w_block(owner, other_half),
               ws_s.at[4 + s - 1], ws_r.at[4 + s - 1], sibling).wait_recv()

    sum_a[...] = jnp.zeros((ROWS, LANES), F32)
    sum_b[...] = jnp.zeros((ROWS, LANES), F32)
    for n in range(4):
        grad = lax.dot_general(cot[...], w_all[n * 256:(n + 1) * 256, :], (((1,), (1,)), ((), ())),
                               preferred_element_type=F32)
        for i in range(2):
            c = 2 * n + i
            grad_normed = grad[:, i * LANES:(i + 1) * LANES] * dfac[c]
            gwin[c, HALO:HALO + ROWS, :] = grad_normed
            sum_a[...] += grad_normed
            sum_b[...] += grad_normed * normed[c]
    sum_a[...] = jnp.broadcast_to(jnp.sum(sum_a[...], axis=1, keepdims=True) * (1.0 / D), (ROWS, LANES))
    sum_b[...] = jnp.broadcast_to(jnp.sum(sum_b[...], axis=1, keepdims=True) * (1.0 / D), (ROWS, LANES))

    def norm_back(c, carry):
        gwin[c, HALO:HALO + ROWS, :] = inv_b[...] * (
            gwin[c, HALO:HALO + ROWS, :] - sum_a[...] - normed[c] * sum_b[...])
        return carry

    lax.fori_loop(0, N, norm_back, 0)

    ghalo_down = remote(gwin.at[:, ROWS:ROWS + HALO, :], gwin.at[:, 0:HALO, :],
                        ghalo_s.at[0], ghalo_r.at[0], next_dev)
    ghalo_up = remote(gwin.at[:, HALO:2 * HALO, :], gwin.at[:, ROWS + HALO:WIN, :],
                      ghalo_s.at[1], ghalo_r.at[1], prev_dev)
    ghalo_down.start()
    ghalo_up.start()

    for n in range(4):
        cols = slice(n * 256, (n + 1) * 256)
        out[:, cols] = jnp.dot(swished[...], w_all[:, cols], preferred_element_type=F32).astype(BF16)
    writes = [pltpu.make_async_copy(out, out_h, done_s.at[0])]
    writes[0].start()

    def backward_pair(p, first, count, stride):
        def body(group, carry):
            base = pl.multiple_of(first + group * stride, GROUP)
            pair = convolve(gwin, (2 * p, 2 * p + 1), base, True)
            for i in range(2):
                c = 2 * p + i
                fgrad[pl.ds(base, GROUP), c * LANES:(c + 1) * LANES] = pair[i].astype(BF16)
            return carry

        lax.fori_loop(0, count, body, 0)

    def reduce_a():
        for k in range(1, N):
            remote(tx1.at[0], rx1.at[k - 1], r1_s.at[k - 1], r1_r.at[k - 1], a_peer(N - k)).wait_recv()
        for c in range(N):
            cols = slice(c * LANES, (c + 1) * LANES)
            total = tx1[a, :, cols].astype(F32)
            for k in range(1, N):
                total = total + rx1[k - 1, :, cols].astype(F32)
            acc2[:, c] = total.reshape(N, 8, LANES)
        for i in range(N):
            tx2[i] = acc2[i].reshape(64, LANES).astype(BF16)
        for k in order:
            remote(tx2.at[(b + k) % N], rx2.at[k - 1], r2_s.at[k - 1], r2_r.at[k - 1], b_peer(k)).start()

    def reduce_b():
        for k in range(1, N):
            remote(tx2.at[0], rx2.at[k - 1], r2_s.at[k - 1], r2_r.at[k - 1], b_peer(N - k)).wait_recv()
        total = acc2[b].reshape(64, LANES)
        for k in range(1, N):
            total = total + rx2[k - 1].astype(F32)
        tx3[...] = total.reshape(N, 8, LANES)
        for k in order:
            remote(tx3.at[(y + k) % N], rx3.at[k - 1], r3_s.at[k - 1], r3_r.at[k - 1], y_peer(k)).start()

    def reduce_y():
        for k in range(1, N):
            remote(tx3.at[0], rx3.at[k - 1], r3_s.at[k - 1], r3_r.at[k - 1], y_peer(N - k)).wait_recv()
        total = tx3[y]
        for k in range(1, N):
            total = total + rx3[k - 1]
        pgrad[...] = total * (1.0 / 1024)
        writes.append(pltpu.make_async_copy(pgrad, pgrad_h, done_s.at[5]))
        writes[-1].start()

    for p in range(4):
        backward_pair(p, GROUP, 2, GROUP)
    reduce_a()
    ghalo_down.wait_recv()
    ghalo_up.wait_recv()
    for p in range(4):
        backward_pair(p, 0, 2, ROWS - GROUP)
        cols = slice(p * 256, (p + 1) * 256)
        writes.append(pltpu.make_async_copy(fgrad.at[:, cols], fgrad_h.at[:, cols], done_s.at[1 + p]))
        writes[-1].start()
    reduce_b()
    reduce_y()

    for k in range(1, N):
        tap_copies[k].wait_send()
        gain_copies[k].wait_send()
        r1[k].wait_send()
        remote(tx2.at[0], rx2.at[k - 1], r2_s.at[k - 1], r2_r.at[k - 1], b_peer(k)).wait_send()
        remote(tx3.at[0], rx3.at[k - 1], r3_s.at[k - 1], r3_r.at[k - 1], y_peer(k)).wait_send()
    for copy in (halo_down, halo_up, ghalo_down, ghalo_up, cot_copy, swt_copy):
        copy.wait_send()
    for copies in (w_right, w_left, w_side):
        for copy in copies.values():
            copy.wait_send()
    for write in writes:
        write.wait()


def deliver(out, fgrad, pgrad, out_to, fgrad_to, pgrad_to):
    out_to[...] = out[...]
    fgrad_to[...] = fgrad[...]
    pgrad_to[...] = pgrad[...]


def per_device(frames, lengths, taps, conv_bias, norm_gain, proj_weight, cotangent):
    dma = pltpu.SemaphoreType.DMA
    hbm = pl.BlockSpec(memory_space=pltpu.HBM)
    shapes = (
        jax.ShapeDtypeStruct((ROWS, D), BF16),
        jax.ShapeDtypeStruct((ROWS, D), BF16),
        jax.ShapeDtypeStruct((8, LANES), F32),
    )
    scratch = [
        pltpu.VMEM((ROWS, D), BF16), pltpu.VMEM((ROWS, D), BF16), pltpu.VMEM((8, LANES), F32),
        pltpu.VMEM((ROWS, D), BF16), pltpu.VMEM((N, LANES), jnp.int32), pltpu.VMEM((TAPS, LANES), BF16),
        pltpu.VMEM((1, LANES), BF16), pltpu.VMEM((1, LANES), BF16), pltpu.VMEM((ROWS, D), BF16),
        pltpu.VMEM((32, LANES), BF16), pltpu.VMEM((16, LANES), BF16), pltpu.VMEM((32, LANES), F32),
        pltpu.VMEM((N, 32, LANES), BF16), pltpu.VMEM((N, 16, LANES), BF16),
        pltpu.VMEM((N, 32, LANES), F32), pltpu.VMEM((N, 16, LANES), F32),
        pltpu.VMEM((2, HALO, D), BF16),
        pltpu.VMEM((N, WIN, LANES), F32), pltpu.VMEM((N, WIN, LANES), F32),
        pltpu.VMEM((ROWS, LANES), F32), pltpu.VMEM((ROWS, LANES), F32),
        pltpu.VMEM((N, ROWS, LANES), F32), pltpu.VMEM((N, ROWS, LANES), F32),
        pltpu.VMEM((N, ROWS, LANES), F32),
        pltpu.VMEM((ROWS, LANES), F32), pltpu.VMEM((ROWS, LANES), F32), pltpu.VMEM((ROWS, LANES), F32),
        pltpu.VMEM((ROWS, D), BF16),
        pltpu.VMEM((2, N, 64, ROWS), BF16), pltpu.VMEM((N, N, 8, ROWS), F32), pltpu.VMEM((N, 64, ROWS), BF16),
        pltpu.VMEM((ROWS, D), BF16), pltpu.VMEM((D, D), BF16),
        pltpu.VMEM((N, 64, D), BF16), pltpu.VMEM((N - 1, 64, D), BF16),
        pltpu.VMEM((N, N, 8, LANES), F32),
        pltpu.VMEM((N, 64, LANES), BF16), pltpu.VMEM((N - 1, 64, LANES), BF16),
        pltpu.VMEM((N, 8, LANES), F32), pltpu.VMEM((N - 1, 8, LANES), F32),
        dma((7,)), dma((7,)), dma((7,)), dma((7,)), dma((2,)), dma((2,)), dma((2,)), dma((2,)),
        dma, dma, dma, dma, dma((4,)), dma((4,)), dma((4,)), dma((4,)), dma((7,)), dma((7,)),
        dma((7,)), dma((7,)), dma((7,)), dma((7,)), dma((7,)), dma((7,)), dma((7,)), dma((6,)),
    ]
    results = pl.pallas_call(
        fused,
        out_shape=shapes,
        in_specs=[hbm] * 7,
        out_specs=(hbm,) * 3,
        scratch_shapes=scratch,
        compiler_params=pltpu.CompilerParams(
            collective_id=0, has_side_effects=True, vmem_limit_bytes=56 * 1024 * 1024),
        name="fused_module",
    )(frames, lengths.reshape(N, LANES), taps, conv_bias.reshape(1, LANES),
      norm_gain.reshape(1, LANES), proj_weight, cotangent)
    vmem = pl.BlockSpec(memory_space=pltpu.VMEM)
    return pl.pallas_call(
        deliver,
        out_shape=shapes,
        in_specs=[vmem] * 3,
        out_specs=(vmem,) * 3,
        name="deliver",
    )(*results)


def solution(mesh):
    rows = P(("dp", "fsdp"), None)
    in_specs = (rows, P(), P(None, "fsdp"), P("fsdp"), P("fsdp"), P(None, "fsdp"), rows)
    out_specs = (rows, rows, P("dp", "fsdp"))
    return jax.shard_map(
        per_device, mesh=mesh, in_specs=in_specs, out_specs=out_specs, check_vma=False)
```

```python
import jax
import jax.numpy as jnp
from jax import lax
from jax.experimental import pallas as pl
from jax.experimental.pallas import tpu as pltpu
from jax.sharding import PartitionSpec as P

MESH = pl.DeviceIdType.MESH
F32 = jnp.float32
BF16 = jnp.bfloat16
N = 8
LANES = 128
ROWS = 256
D = 1024
TAPS = 31
HALO = 16
WIN = ROWS + 2 * HALO
GROUP = 64


def fused(frames_h, lengths_h, taps_h, bias_h, gain_h, weight, cot_h,
          out, fgrad, pgrad,
          frames, lengths, taps, bias, gain, cot,
          pack, gpack, pack_f, tap_all, gain_all, tap_f, gain_f,
          halo, fwin, gwin, off_b, rem_b,
          conv, normed, dfac, inv_b, sum_a, sum_b,
          swished, swt, swt_f, swt_rx, cot_sib, w_all,
          tx1, rx1, acc2, tx2, rx2, tx3, rx3,
          tap_s, tap_r, gain_s, gain_r, halo_s, halo_r, ghalo_s, ghalo_r,
          cot_s, cot_r, swt_s, swt_r, wr_s, wr_r, wl_s, wl_r, ws_s, ws_r,
          r1_s, r1_r, r2_s, r2_r, r3_s, r3_r, loc_s):
    dp = lax.axis_index("dp")
    y = lax.axis_index("fsdp")
    core = dp % 2
    z = (dp // 2) % N
    x = dp // (2 * N)
    a = x * (1 - core) + z * core
    b = z * (1 - core) + x * core

    def chip(a_to, b_to):
        return (a_to * (N - (N - 1) * core) + b_to * (1 + (N - 1) * core)) * 2 + core

    def y_peer(k):
        return (dp, (y + k) % N)

    def a_peer(k):
        return (chip((a + k) % N, b), y)

    def b_peer(k):
        return (chip(a, (b + k) % N), y)

    sibling = (dp + 1 - 2 * core, y)
    place = dp * N + y
    count = 128 * N
    after = (place + 1) % count
    before = (place + count - 1) % count
    next_dev = (after // N, after % N)
    prev_dev = (before // N, before % N)

    def remote(src, dst, send, recv, to):
        return pltpu.make_async_remote_copy(
            src_ref=src, dst_ref=dst, send_sem=send, recv_sem=recv,
            device_id=to, device_id_type=MESH)

    loads = [pltpu.make_async_copy(src, dst, loc_s.at[i]) for i, (src, dst) in enumerate((
        (lengths_h, lengths), (taps_h, taps), (bias_h, bias), (gain_h, gain), (frames_h, frames), (cot_h, cot)))]
    for load in loads:
        load.start()

    barrier = pltpu.get_barrier_semaphore()
    order = (4, 3, 5, 2, 6, 1, 7)
    peers = [y_peer(k) for k in order] + [next_dev, prev_dev, sibling]
    for k in order:
        peers += [a_peer(k), b_peer(k)]
    for peer in peers:
        pl.semaphore_signal(barrier, inc=1, device_id=peer, device_id_type=MESH)

    for load in loads[:4]:
        load.wait()

    pack_f[0:TAPS, :] = taps[...].astype(F32)
    pack_f[TAPS:TAPS + 1, :] = bias[...].astype(F32)
    pack[...] = pack_f[...].astype(BF16)
    gpack[...] = jnp.broadcast_to(gain[...].astype(F32), (16, LANES)).astype(BF16)

    pl.semaphore_wait(barrier, len(peers))

    near = (1, 7, 2, 6, 3, 5, 4)
    tap_copies = {}
    gain_copies = {}
    for k in near:
        tap_copies[k] = remote(pack, tap_all.at[y], tap_s.at[k - 1], tap_r.at[k - 1], y_peer(k))
        tap_copies[k].start()
    halo_down = remote(frames_h.at[ROWS - HALO:ROWS], halo.at[0], halo_s.at[0], halo_r.at[0], next_dev)
    halo_up = remote(frames_h.at[0:HALO], halo.at[1], halo_s.at[1], halo_r.at[1], prev_dev)
    halo_down.start()
    halo_up.start()
    half = D // 2
    my_half = pl.ds(pl.multiple_of(core * half, half), half)
    other_half = pl.ds(pl.multiple_of((1 - core) * half, half), half)

    def shard(owner):
        return pl.ds(pl.multiple_of(owner * LANES, LANES), LANES)

    def w_block(owner, rows):
        return w_all.at[rows, shard(owner)]

    right, left = y_peer(1), y_peer(N - 1)
    w_right, w_left, w_side = {}, {}, {}

    quarter = half // 2
    first_part = pl.ds(pl.multiple_of(core * half, quarter), quarter)
    second_part = pl.ds(pl.multiple_of(core * half + quarter, quarter), quarter)

    def send_right(s):
        owner = (y - (s - 1) + N) % N
        rows = first_part if s == 4 else my_half
        src = weight.at[rows, :] if s == 1 else w_block(owner, rows)
        w_right[s] = remote(src, w_block(owner, rows), wr_s.at[s - 1], wr_r.at[s - 1], right)
        w_right[s].start()

    def send_left(s):
        owner = (y + (s - 1)) % N
        rows = second_part if s == 4 else my_half
        src = weight.at[rows, :] if s == 1 else w_block(owner, rows)
        w_left[s] = remote(src, w_block(owner, rows), wl_s.at[s - 1], wl_r.at[s - 1], left)
        w_left[s].start()

    def send_side(slot, owner):
        w_side[slot] = remote(w_block(owner, my_half), w_block(owner, my_half),
                              ws_s.at[slot], ws_r.at[slot], sibling)
        w_side[slot].start()

    def w_service(s):
        below, above = (y - s + N) % N, (y + s) % N
        rows = first_part if s == 4 else my_half
        remote(w_block(below, rows), w_block(below, rows), wr_s.at[s - 1], wr_r.at[s - 1], right).wait_recv()
        if s < 4:
            send_right(s + 1)
            send_side(s - 1, below)
        rows = second_part if s == 4 else my_half
        remote(w_block(above, rows), w_block(above, rows), wl_s.at[s - 1], wl_r.at[s - 1], left).wait_recv()
        if s < 4:
            send_left(s + 1)
            send_side(3 + s, above)
        else:
            send_side(3, below)

    for k in near:
        gain_copies[k] = remote(gpack, gain_all.at[y], gain_s.at[k - 1], gain_r.at[k - 1], y_peer(k))
        gain_copies[k].start()
    send_right(1)
    send_left(1)
    cot_copy = remote(cot_h, cot_sib, cot_s, cot_r, sibling)
    cot_copy.start()
    own_w = pltpu.make_async_copy(weight, w_all.at[:, shard(y)], loc_s.at[6])
    own_w.start()

    ends = lengths[...].astype(F32)
    lane = lax.broadcasted_iota(jnp.int32, (N, LANES), 1)
    row8 = lax.broadcasted_iota(jnp.int32, (N, LANES), 0)
    step = 1
    while step < LANES:
        ends = ends + jnp.where(lane >= step, pltpu.roll(ends, step, 1), 0.0)
        step *= 2
    total = jnp.broadcast_to(jnp.max(ends, axis=1, keepdims=True), (N, LANES))
    before_sum = jnp.where(row8 >= 1, pltpu.roll(total, 1, 0), 0.0)
    step = 1
    while step < N:
        before_sum = before_sum + jnp.where(row8 >= step, pltpu.roll(before_sum, step, 0), 0.0)
        step *= 2
    ends = ends + before_sum - (place * ROWS).astype(F32)
    acc2[0, 0] = ends

    def locate(group, carry):
        base = pl.multiple_of(group * GROUP, GROUP)
        rows = (lax.broadcasted_iota(jnp.int32, (GROUP, LANES), 0) + base).astype(F32)
        start = jnp.full((GROUP, LANES), -1e9, F32)
        stop = jnp.full((GROUP, LANES), 1e9, F32)
        for i in range(N):
            edge = jnp.broadcast_to(acc2[0, 0, i:i + 1, :], (GROUP, LANES))
            passed = edge <= rows
            start = jnp.maximum(start, jnp.where(passed, edge, -1e9))
            stop = jnp.minimum(stop, jnp.where(passed, 1e9, edge))
        first = (-(place * ROWS)).astype(F32)
        start = jnp.maximum(jnp.max(start, axis=1, keepdims=True), first)
        stop = jnp.min(stop, axis=1, keepdims=True)
        off_b[pl.ds(base, GROUP), :] = rows - start
        rem_b[pl.ds(base, GROUP), :] = stop - rows
        return carry

    lax.fori_loop(0, ROWS // GROUP, locate, 0)

    loads[4].wait()
    for c in range(N):
        fwin[c, HALO:HALO + ROWS, :] = frames[:, c * LANES:(c + 1) * LANES].astype(F32)

    def tap_arrives(k):
        source = (y - k + N) % N
        remote(tap_all.at[source], tap_all.at[source], tap_s.at[k - 1], tap_r.at[k - 1],
               y_peer(N - k)).wait_recv()
        tap_f[source] = tap_all[source].astype(F32)
        return source

    def convolve(window, blocks, base, reverse):
        off = off_b[pl.ds(base, GROUP), :]
        rem = rem_b[pl.ds(base, GROUP), :]
        sums = []
        for c in blocks:
            if reverse:
                sums.append(jnp.zeros((GROUP, LANES), F32))
            else:
                sums.append(jnp.broadcast_to(tap_f[c, TAPS:TAPS + 1, :], (GROUP, LANES)))
        for j in range(TAPS):
            d = j - (TAPS - 1) // 2
            together = off >= float(-d) if d < 0 else rem > float(d)
            tap = TAPS - 1 - j if reverse else j
            for i, c in enumerate(blocks):
                value = window[c, pl.ds(base + (j + 1), GROUP), :]
                if d != 0:
                    value = jnp.where(together, value, 0.0)
                sums[i] = sums[i] + tap_f[c, tap:tap + 1, :] * value
        return sums

    def forward_blocks(blocks, first, count, stride):
        def body(group, carry):
            base = pl.multiple_of(first + group * stride, GROUP)
            for c, value in zip(blocks, convolve(fwin, blocks, base, False)):
                conv[c, pl.ds(base, GROUP), :] = value
            return carry

        lax.fori_loop(0, count, body, 0)

    tap_f[y] = pack[...].astype(F32)
    forward_blocks((y,), GROUP, 2, GROUP)
    blocks = (tap_arrives(1), tap_arrives(7))
    forward_blocks(blocks, GROUP, 2, GROUP)
    halo_down.wait_recv()
    halo_up.wait_recv()
    for c in range(N):
        fwin[c, 0:HALO, :] = halo[0, :, c * LANES:(c + 1) * LANES].astype(F32)
        fwin[c, HALO + ROWS:WIN, :] = halo[1, :, c * LANES:(c + 1) * LANES].astype(F32)
    forward_blocks(blocks, 0, 2, ROWS - GROUP)
    forward_blocks((tap_arrives(2), tap_arrives(6)), 0, 4, GROUP)
    w_service(1)
    forward_blocks((tap_arrives(3), tap_arrives(5)), 0, 4, GROUP)
    last = tap_arrives(4)
    forward_blocks((y, last), 0, 2, ROWS - GROUP)
    forward_blocks((last,), GROUP, 2, GROUP)

    def over_features(make):
        def body(group, carry):
            base = pl.multiple_of(group * GROUP, GROUP)
            rows = pl.ds(base, GROUP)
            sum_a[rows, :] = make(rows)
            return carry

        lax.fori_loop(0, ROWS // GROUP, body, 0)
        return jnp.sum(sum_a[...], axis=1, keepdims=True) * (1.0 / D)

    def plain(rows):
        total = conv[0, rows, :]
        for c in range(1, N):
            total = total + conv[c, rows, :]
        return total

    sum_b[...] = jnp.broadcast_to(over_features(plain), (ROWS, LANES))

    def squares(rows):
        mean = sum_b[rows, :]
        total = jnp.zeros((GROUP, LANES), F32)
        for c in range(N):
            centre = conv[c, rows, :] - mean
            total = total + centre * centre
        return total

    inv_b[...] = jnp.broadcast_to(lax.rsqrt(over_features(squares) + 1e-05), (ROWS, LANES))

    gain_f[y] = gpack[...].astype(F32)
    for k in range(1, N):
        source = (y - k + N) % N
        remote(gain_all.at[source], gain_all.at[source], gain_s.at[k - 1], gain_r.at[k - 1],
               y_peer(N - k)).wait_recv()
        gain_f[source] = gain_all[source].astype(F32)

    def swish_block(c, carry):
        gain_row = gain_f[c, 0:1, :]
        for h in range(2):
            rows = pl.ds(h * 128, 128)
            unit = (conv[c, rows, :] - sum_b[rows, :]) * inv_b[rows, :]
            normed[c, rows, :] = unit
            scaled = unit * gain_row
            gate = 1.0 / (1.0 + jnp.exp(-scaled))
            sw = (scaled * gate).astype(BF16)
            dfac[c, rows, :] = (gate + scaled * gate * (1.0 - gate)) * gain_row
            swished[rows, shard(c)] = sw
            turned = jnp.transpose(sw.astype(F32)).reshape(N, 2, 8, 128)
            swt[0, c, :, h * 128:(h + 1) * 128] = turned[:, 0].reshape(64, 128).astype(BF16)
            swt_f[:, c, :, h * 128:(h + 1) * 128] = turned[:, 1]
        return carry

    lax.fori_loop(0, N, swish_block, 0)
    for i in range(N):
        swt[1, i] = swt_f[i].reshape(64, ROWS).astype(BF16)

    swt_copy = remote(swt.at[1 - core], swt_rx, swt_s, swt_r, sibling)
    swt_copy.start()
    w_service(2)
    loads[5].wait()
    cot_copy.wait_recv()
    swt_copy.wait_recv()

    for n in range(4):
        cols = slice(n * 256, (n + 1) * 256)
        part = jnp.dot(swt[core].reshape(512, ROWS), cot[:, cols], preferred_element_type=F32)
        part = part + jnp.dot(swt_rx[...].reshape(512, ROWS), cot_sib[:, cols], preferred_element_type=F32)
        tx1[:, :, cols] = part.astype(BF16).reshape(N, 64, 256)

    r1 = {}
    for k in order:
        r1[k] = remote(tx1.at[(a + k) % N], rx1.at[k - 1], r1_s.at[k - 1], r1_r.at[k - 1], a_peer(k))
        r1[k].start()

    w_service(3)
    w_service(4)
    own_w.wait()
    for s in range(1, 5):
        owner = (y - s + N) % N
        remote(w_block(owner, other_half), w_block(owner, other_half),
               ws_s.at[s - 1], ws_r.at[s - 1], sibling).wait_recv()
    for s in range(1, 4):
        owner = (y + s) % N
        remote(w_block(owner, other_half), w_block(owner, other_half),
               ws_s.at[4 + s - 1], ws_r.at[4 + s - 1], sibling).wait_recv()

    sum_a[...] = jnp.zeros((ROWS, LANES), F32)
    sum_b[...] = jnp.zeros((ROWS, LANES), F32)
    for n in range(4):
        grad = lax.dot_general(cot[...], w_all[n * 256:(n + 1) * 256, :], (((1,), (1,)), ((), ())),
                               preferred_element_type=F32)
        for i in range(2):
            c = 2 * n + i
            grad_normed = grad[:, i * LANES:(i + 1) * LANES] * dfac[c]
            gwin[c, HALO:HALO + ROWS, :] = grad_normed
            sum_a[...] += grad_normed
            sum_b[...] += grad_normed * normed[c]
    sum_a[...] = jnp.broadcast_to(jnp.sum(sum_a[...], axis=1, keepdims=True) * (1.0 / D), (ROWS, LANES))
    sum_b[...] = jnp.broadcast_to(jnp.sum(sum_b[...], axis=1, keepdims=True) * (1.0 / D), (ROWS, LANES))

    def norm_back(c, carry):
        gwin[c, HALO:HALO + ROWS, :] = inv_b[...] * (
            gwin[c, HALO:HALO + ROWS, :] - sum_a[...] - normed[c] * sum_b[...])
        return carry

    lax.fori_loop(0, N, norm_back, 0)

    ghalo_down = remote(gwin.at[:, ROWS:ROWS + HALO, :], gwin.at[:, 0:HALO, :],
                        ghalo_s.at[0], ghalo_r.at[0], next_dev)
    ghalo_up = remote(gwin.at[:, HALO:2 * HALO, :], gwin.at[:, ROWS + HALO:WIN, :],
                      ghalo_s.at[1], ghalo_r.at[1], prev_dev)
    ghalo_down.start()
    ghalo_up.start()

    for n in range(4):
        cols = slice(n * 256, (n + 1) * 256)
        out[:, cols] = jnp.dot(swished[...], w_all[:, cols], preferred_element_type=F32).astype(BF16)

    def backward_pair(p, first, count, stride):
        def body(group, carry):
            base = pl.multiple_of(first + group * stride, GROUP)
            pair = convolve(gwin, (2 * p, 2 * p + 1), base, True)
            for i in range(2):
                c = 2 * p + i
                fgrad[pl.ds(base, GROUP), c * LANES:(c + 1) * LANES] = pair[i].astype(BF16)
            return carry

        lax.fori_loop(0, count, body, 0)

    def reduce_a():
        for k in range(1, N):
            remote(tx1.at[0], rx1.at[k - 1], r1_s.at[k - 1], r1_r.at[k - 1], a_peer(N - k)).wait_recv()
        for c in range(N):
            cols = slice(c * LANES, (c + 1) * LANES)
            total = tx1[a, :, cols].astype(F32)
            for k in range(1, N):
                total = total + rx1[k - 1, :, cols].astype(F32)
            acc2[:, c] = total.reshape(N, 8, LANES)
        for i in range(N):
            tx2[i] = acc2[i].reshape(64, LANES).astype(BF16)
        for k in order:
            remote(tx2.at[(b + k) % N], rx2.at[k - 1], r2_s.at[k - 1], r2_r.at[k - 1], b_peer(k)).start()

    def reduce_b():
        for k in range(1, N):
            remote(tx2.at[0], rx2.at[k - 1], r2_s.at[k - 1], r2_r.at[k - 1], b_peer(N - k)).wait_recv()
        total = acc2[b].reshape(64, LANES)
        for k in range(1, N):
            total = total + rx2[k - 1].astype(F32)
        tx3[...] = total.reshape(N, 8, LANES)
        for k in order:
            remote(tx3.at[(y + k) % N], rx3.at[k - 1], r3_s.at[k - 1], r3_r.at[k - 1], y_peer(k)).start()

    def reduce_y():
        for k in range(1, N):
            remote(tx3.at[0], rx3.at[k - 1], r3_s.at[k - 1], r3_r.at[k - 1], y_peer(N - k)).wait_recv()
        total = tx3[y]
        for k in range(1, N):
            total = total + rx3[k - 1]
        pgrad[...] = total * (1.0 / 1024)

    for p in range(4):
        backward_pair(p, GROUP, 2, GROUP)
    reduce_a()
    ghalo_down.wait_recv()
    ghalo_up.wait_recv()
    for p in range(4):
        backward_pair(p, 0, 2, ROWS - GROUP)
    reduce_b()
    reduce_y()

    for k in range(1, N):
        tap_copies[k].wait_send()
        gain_copies[k].wait_send()
        r1[k].wait_send()
        remote(tx2.at[0], rx2.at[k - 1], r2_s.at[k - 1], r2_r.at[k - 1], b_peer(k)).wait_send()
        remote(tx3.at[0], rx3.at[k - 1], r3_s.at[k - 1], r3_r.at[k - 1], y_peer(k)).wait_send()
    for copy in (halo_down, halo_up, ghalo_down, ghalo_up, cot_copy, swt_copy):
        copy.wait_send()
    for copies in (w_right, w_left, w_side):
        for copy in copies.values():
            copy.wait_send()


def deliver(out, fgrad, pgrad, out_to, fgrad_to, pgrad_to, sem):
    copies = [pltpu.make_async_copy(src, dst, sem.at[i]) for i, (src, dst) in enumerate(
        ((out, out_to), (fgrad, fgrad_to), (pgrad, pgrad_to)))]
    for copy in copies:
        copy.start()
    for copy in copies:
        copy.wait()


def per_device(frames, lengths, taps, conv_bias, norm_gain, proj_weight, cotangent):
    dma = pltpu.SemaphoreType.DMA
    vmem = pl.BlockSpec(memory_space=pltpu.VMEM)
    hbm = pl.BlockSpec(memory_space=pltpu.HBM)
    shapes = (
        jax.ShapeDtypeStruct((ROWS, D), BF16),
        jax.ShapeDtypeStruct((ROWS, D), BF16),
        jax.ShapeDtypeStruct((8, LANES), F32),
    )
    scratch = [
        pltpu.VMEM((ROWS, D), BF16), pltpu.VMEM((N, LANES), jnp.int32), pltpu.VMEM((TAPS, LANES), BF16),
        pltpu.VMEM((1, LANES), BF16), pltpu.VMEM((1, LANES), BF16), pltpu.VMEM((ROWS, D), BF16),
        pltpu.VMEM((32, LANES), BF16), pltpu.VMEM((16, LANES), BF16), pltpu.VMEM((32, LANES), F32),
        pltpu.VMEM((N, 32, LANES), BF16), pltpu.VMEM((N, 16, LANES), BF16),
        pltpu.VMEM((N, 32, LANES), F32), pltpu.VMEM((N, 16, LANES), F32),
        pltpu.VMEM((2, HALO, D), BF16),
        pltpu.VMEM((N, WIN, LANES), F32), pltpu.VMEM((N, WIN, LANES), F32),
        pltpu.VMEM((ROWS, LANES), F32), pltpu.VMEM((ROWS, LANES), F32),
        pltpu.VMEM((N, ROWS, LANES), F32), pltpu.VMEM((N, ROWS, LANES), F32),
        pltpu.VMEM((N, ROWS, LANES), F32),
        pltpu.VMEM((ROWS, LANES), F32), pltpu.VMEM((ROWS, LANES), F32), pltpu.VMEM((ROWS, LANES), F32),
        pltpu.VMEM((ROWS, D), BF16),
        pltpu.VMEM((2, N, 64, ROWS), BF16), pltpu.VMEM((N, N, 8, ROWS), F32), pltpu.VMEM((N, 64, ROWS), BF16),
        pltpu.VMEM((ROWS, D), BF16), pltpu.VMEM((D, D), BF16),
        pltpu.VMEM((N, 64, D), BF16), pltpu.VMEM((N - 1, 64, D), BF16),
        pltpu.VMEM((N, N, 8, LANES), F32),
        pltpu.VMEM((N, 64, LANES), BF16), pltpu.VMEM((N - 1, 64, LANES), BF16),
        pltpu.VMEM((N, 8, LANES), F32), pltpu.VMEM((N - 1, 8, LANES), F32),
        dma((7,)), dma((7,)), dma((7,)), dma((7,)), dma((2,)), dma((2,)), dma((2,)), dma((2,)),
        dma, dma, dma, dma, dma((4,)), dma((4,)), dma((4,)), dma((4,)), dma((7,)), dma((7,)),
        dma((7,)), dma((7,)), dma((7,)), dma((7,)), dma((7,)), dma((7,)), dma((7,)),
    ]
    results = pl.pallas_call(
        fused,
        out_shape=shapes,
        in_specs=[hbm] * 7,
        out_specs=(vmem,) * 3,
        scratch_shapes=scratch,
        compiler_params=pltpu.CompilerParams(
            collective_id=0, has_side_effects=True, vmem_limit_bytes=40 * 1024 * 1024),
        name="fused_module",
    )(*(pltpu.with_memory_space_constraint(value, pltpu.HBM) for value in (
        frames, lengths.reshape(N, LANES), taps, conv_bias.reshape(1, LANES),
        norm_gain.reshape(1, LANES), proj_weight, cotangent)))
    return pl.pallas_call(
        deliver,
        out_shape=shapes,
        in_specs=[vmem] * 3,
        out_specs=(hbm,) * 3,
        scratch_shapes=[dma((3,))],
        name="deliver",
    )(*(pltpu.with_memory_space_constraint(value, pltpu.VMEM) for value in results))


def solution(mesh):
    rows = P(("dp", "fsdp"), None)
    in_specs = (rows, P(), P(None, "fsdp"), P("fsdp"), P("fsdp"), P(None, "fsdp"), rows)
    out_specs = (rows, rows, P("dp", "fsdp"))
    return jax.shard_map(
        per_device, mesh=mesh, in_specs=in_specs, out_specs=out_specs, check_vma=False)
```

```python
import jax
import jax.numpy as jnp
from jax import lax
from jax.experimental import pallas as pl
from jax.experimental.pallas import tpu as pltpu
from jax.sharding import PartitionSpec as P

MESH = pl.DeviceIdType.MESH
F32 = jnp.float32
BF16 = jnp.bfloat16
N = 8
LANES = 128
ROWS = 256
D = 1024
TAPS = 31
HALO = 16
WIN = ROWS + 2 * HALO
GROUP = 64
EARLY = 16


def fused(frames_h, lengths_h, taps_h, bias_h, gain_h, weight, cot_h,
          out, fgrad, pgrad,
          frames, lengths, taps, bias, gain, cot,
          pack, gpack, pack_f, tap_all, gain_all, tap_f, gain_f,
          halo, fwin, gwin, off_b, rem_b,
          conv, normed, dfac, inv_b, sum_a, sum_b,
          swished, swt, swt_f, swt_rx, cot_sib, w_all,
          tx1, rx1, acc2, tx2, rx2, tx3, rx3, rxy, txa, rxa, txb, rxb,
          tap_s, tap_r, gain_s, gain_r, halo_s, halo_r, ghalo_s, ghalo_r,
          cot_s, cot_r, swt_s, swt_r, wr_s, wr_r, wl_s, wl_r, ws_s, ws_r,
          r1_s, r1_r, r2_s, r2_r, r3_s, r3_r, ry_s, ry_r, ra_s, ra_r, rb_s, rb_r, loc_s):
    dp = lax.axis_index("dp")
    y = lax.axis_index("fsdp")
    core = dp % 2
    z = (dp // 2) % N
    x = dp // (2 * N)
    a = x * (1 - core) + z * core
    b = z * (1 - core) + x * core

    def chip(a_to, b_to):
        return (a_to * (N - (N - 1) * core) + b_to * (1 + (N - 1) * core)) * 2 + core

    def y_peer(k):
        return (dp, (y + k) % N)

    def a_peer(k):
        return (chip((a + k) % N, b), y)

    def b_peer(k):
        return (chip(a, (b + k) % N), y)

    sibling = (dp + 1 - 2 * core, y)
    place = dp * N + y
    count = 128 * N
    after = (place + 1) % count
    before = (place + count - 1) % count
    next_dev = (after // N, after % N)
    prev_dev = (before // N, before % N)

    def remote(src, dst, send, recv, to):
        return pltpu.make_async_remote_copy(
            src_ref=src, dst_ref=dst, send_sem=send, recv_sem=recv,
            device_id=to, device_id_type=MESH)

    loads = [pltpu.make_async_copy(src, dst, loc_s.at[i]) for i, (src, dst) in enumerate((
        (lengths_h, lengths), (taps_h, taps), (bias_h, bias), (gain_h, gain), (frames_h, frames), (cot_h, cot)))]
    for load in loads:
        load.start()

    barrier = pltpu.get_barrier_semaphore()
    order = (4, 3, 5, 2, 6, 1, 7)
    peers = [y_peer(k) for k in order] + [next_dev, prev_dev, sibling]
    for k in order:
        peers += [a_peer(k), b_peer(k)]
    for peer in peers:
        pl.semaphore_signal(barrier, inc=1, device_id=peer, device_id_type=MESH)

    for load in loads[:4]:
        load.wait()

    pack_f[0:TAPS, :] = taps[...].astype(F32)
    pack_f[TAPS:TAPS + 1, :] = bias[...].astype(F32)
    pack[...] = pack_f[...].astype(BF16)
    gpack[...] = jnp.broadcast_to(gain[...].astype(F32), (16, LANES)).astype(BF16)

    pl.semaphore_wait(barrier, len(peers))

    near = (1, 7, 2, 6, 3, 5, 4)
    tap_copies = {}
    gain_copies = {}
    for k in near:
        tap_copies[k] = remote(pack, tap_all.at[y], tap_s.at[k - 1], tap_r.at[k - 1], y_peer(k))
        tap_copies[k].start()
    halo_down = remote(frames_h.at[ROWS - HALO:ROWS], halo.at[0], halo_s.at[0], halo_r.at[0], next_dev)
    halo_up = remote(frames_h.at[0:HALO], halo.at[1], halo_s.at[1], halo_r.at[1], prev_dev)
    halo_down.start()
    halo_up.start()
    half = D // 2
    my_half = pl.ds(pl.multiple_of(core * half, half), half)
    other_half = pl.ds(pl.multiple_of((1 - core) * half, half), half)

    def shard(owner):
        return pl.ds(pl.multiple_of(owner * LANES, LANES), LANES)

    def w_block(owner, rows):
        return w_all.at[rows, shard(owner)]

    right, left = y_peer(1), y_peer(N - 1)
    w_right, w_left, w_side = {}, {}, {}

    quarter = half // 2
    first_part = pl.ds(pl.multiple_of(core * half, quarter), quarter)
    second_part = pl.ds(pl.multiple_of(core * half + quarter, quarter), quarter)

    def send_right(s):
        owner = (y - (s - 1) + N) % N
        rows = first_part if s == 4 else my_half
        src = weight.at[rows, :] if s == 1 else w_block(owner, rows)
        w_right[s] = remote(src, w_block(owner, rows), wr_s.at[s - 1], wr_r.at[s - 1], right)
        w_right[s].start()

    def send_left(s):
        owner = (y + (s - 1)) % N
        rows = second_part if s == 4 else my_half
        src = weight.at[rows, :] if s == 1 else w_block(owner, rows)
        w_left[s] = remote(src, w_block(owner, rows), wl_s.at[s - 1], wl_r.at[s - 1], left)
        w_left[s].start()

    def send_side(slot, owner):
        w_side[slot] = remote(w_block(owner, my_half), w_block(owner, my_half),
                              ws_s.at[slot], ws_r.at[slot], sibling)
        w_side[slot].start()

    def w_service(s):
        below, above = (y - s + N) % N, (y + s) % N
        rows = first_part if s == 4 else my_half
        remote(w_block(below, rows), w_block(below, rows), wr_s.at[s - 1], wr_r.at[s - 1], right).wait_recv()
        if s < 4:
            send_right(s + 1)
            send_side(s - 1, below)
        rows = second_part if s == 4 else my_half
        remote(w_block(above, rows), w_block(above, rows), wl_s.at[s - 1], wl_r.at[s - 1], left).wait_recv()
        if s < 4:
            send_left(s + 1)
            send_side(3 + s, above)
        else:
            send_side(3, below)

    for k in near:
        gain_copies[k] = remote(gpack, gain_all.at[y], gain_s.at[k - 1], gain_r.at[k - 1], y_peer(k))
        gain_copies[k].start()
    send_right(1)
    send_left(1)
    cot_copy = remote(cot_h, cot_sib, cot_s, cot_r, sibling)
    cot_copy.start()
    own_w = pltpu.make_async_copy(weight, w_all.at[:, shard(y)], loc_s.at[6])
    own_w.start()

    ends = lengths[...].astype(F32)
    lane = lax.broadcasted_iota(jnp.int32, (N, LANES), 1)
    row8 = lax.broadcasted_iota(jnp.int32, (N, LANES), 0)
    step = 1
    while step < LANES:
        ends = ends + jnp.where(lane >= step, pltpu.roll(ends, step, 1), 0.0)
        step *= 2
    total = jnp.broadcast_to(jnp.max(ends, axis=1, keepdims=True), (N, LANES))
    before_sum = jnp.where(row8 >= 1, pltpu.roll(total, 1, 0), 0.0)
    step = 1
    while step < N:
        before_sum = before_sum + jnp.where(row8 >= step, pltpu.roll(before_sum, step, 0), 0.0)
        step *= 2
    ends = ends + before_sum - (place * ROWS).astype(F32)
    acc2[0, 0] = ends

    def locate(group, carry):
        base = pl.multiple_of(group * GROUP, GROUP)
        rows = (lax.broadcasted_iota(jnp.int32, (GROUP, LANES), 0) + base).astype(F32)
        start = jnp.full((GROUP, LANES), -1e9, F32)
        stop = jnp.full((GROUP, LANES), 1e9, F32)
        for i in range(N):
            edge = jnp.broadcast_to(acc2[0, 0, i:i + 1, :], (GROUP, LANES))
            passed = edge <= rows
            start = jnp.maximum(start, jnp.where(passed, edge, -1e9))
            stop = jnp.minimum(stop, jnp.where(passed, 1e9, edge))
        first = (-(place * ROWS)).astype(F32)
        start = jnp.maximum(jnp.max(start, axis=1, keepdims=True), first)
        stop = jnp.min(stop, axis=1, keepdims=True)
        off_b[pl.ds(base, GROUP), :] = rows - start
        rem_b[pl.ds(base, GROUP), :] = stop - rows
        return carry

    lax.fori_loop(0, ROWS // GROUP, locate, 0)

    loads[4].wait()
    for c in range(N):
        fwin[c, HALO:HALO + ROWS, :] = frames[:, c * LANES:(c + 1) * LANES].astype(F32)

    def tap_arrives(k):
        source = (y - k + N) % N
        remote(tap_all.at[source], tap_all.at[source], tap_s.at[k - 1], tap_r.at[k - 1],
               y_peer(N - k)).wait_recv()
        tap_f[source] = tap_all[source].astype(F32)
        return source

    def convolve(window, blocks, base, reverse):
        off = off_b[pl.ds(base, GROUP), :]
        rem = rem_b[pl.ds(base, GROUP), :]
        sums = []
        for c in blocks:
            if reverse:
                sums.append(jnp.zeros((GROUP, LANES), F32))
            else:
                sums.append(jnp.broadcast_to(tap_f[c, TAPS:TAPS + 1, :], (GROUP, LANES)))
        for j in range(TAPS):
            d = j - (TAPS - 1) // 2
            together = off >= float(-d) if d < 0 else rem > float(d)
            tap = TAPS - 1 - j if reverse else j
            for i, c in enumerate(blocks):
                value = window[c, pl.ds(base + (j + 1), GROUP), :]
                if d != 0:
                    value = jnp.where(together, value, 0.0)
                sums[i] = sums[i] + tap_f[c, tap:tap + 1, :] * value
        return sums

    def forward_blocks(blocks, first, count, stride):
        def body(group, carry):
            base = pl.multiple_of(first + group * stride, GROUP)
            for c, value in zip(blocks, convolve(fwin, blocks, base, False)):
                conv[c, pl.ds(base, GROUP), :] = value
            return carry

        lax.fori_loop(0, count, body, 0)

    tap_f[y] = pack[...].astype(F32)
    forward_blocks((y,), GROUP, 2, GROUP)
    blocks = (tap_arrives(1), tap_arrives(7))
    forward_blocks(blocks, GROUP, 2, GROUP)
    halo_down.wait_recv()
    halo_up.wait_recv()
    for c in range(N):
        fwin[c, 0:HALO, :] = halo[0, :, c * LANES:(c + 1) * LANES].astype(F32)
        fwin[c, HALO + ROWS:WIN, :] = halo[1, :, c * LANES:(c + 1) * LANES].astype(F32)
    forward_blocks(blocks, 0, 2, ROWS - GROUP)
    forward_blocks((tap_arrives(2), tap_arrives(6)), 0, 4, GROUP)
    w_service(1)
    forward_blocks((tap_arrives(3), tap_arrives(5)), 0, 4, GROUP)
    last = tap_arrives(4)
    forward_blocks((y, last), 0, 2, ROWS - GROUP)
    forward_blocks((last,), GROUP, 2, GROUP)

    def over_features(make):
        def body(group, carry):
            base = pl.multiple_of(group * GROUP, GROUP)
            rows = pl.ds(base, GROUP)
            sum_a[rows, :] = make(rows)
            return carry

        lax.fori_loop(0, ROWS // GROUP, body, 0)
        return jnp.sum(sum_a[...], axis=1, keepdims=True) * (1.0 / D)

    def plain(rows):
        total = conv[0, rows, :]
        for c in range(1, N):
            total = total + conv[c, rows, :]
        return total

    sum_b[...] = jnp.broadcast_to(over_features(plain), (ROWS, LANES))

    def squares(rows):
        mean = sum_b[rows, :]
        total = jnp.zeros((GROUP, LANES), F32)
        for c in range(N):
            centre = conv[c, rows, :] - mean
            total = total + centre * centre
        return total

    inv_b[...] = jnp.broadcast_to(lax.rsqrt(over_features(squares) + 1e-05), (ROWS, LANES))

    gain_f[y] = gpack[...].astype(F32)
    for k in range(1, N):
        source = (y - k + N) % N
        remote(gain_all.at[source], gain_all.at[source], gain_s.at[k - 1], gain_r.at[k - 1],
               y_peer(N - k)).wait_recv()
        gain_f[source] = gain_all[source].astype(F32)

    def swish_block(c, carry):
        gain_row = gain_f[c, 0:1, :]
        for h in range(2):
            rows = pl.ds(h * 128, 128)
            unit = (conv[c, rows, :] - sum_b[rows, :]) * inv_b[rows, :]
            normed[c, rows, :] = unit
            scaled = unit * gain_row
            gate = 1.0 / (1.0 + jnp.exp(-scaled))
            sw = (scaled * gate).astype(BF16)
            dfac[c, rows, :] = (gate + scaled * gate * (1.0 - gate)) * gain_row
            swished[rows, shard(c)] = sw
            turned = jnp.transpose(sw.astype(F32)).reshape(N, 2, 8, 128)
            swt[0, c, :, h * 128:(h + 1) * 128] = turned[:, 0].reshape(64, 128).astype(BF16)
            swt_f[:, c, :, h * 128:(h + 1) * 128] = turned[:, 1]
        return carry

    lax.fori_loop(0, N, swish_block, 0)
    for i in range(N):
        swt[1, i] = swt_f[i].reshape(64, ROWS).astype(BF16)

    swt_copy = remote(swt.at[1 - core], swt_rx, swt_s, swt_r, sibling)
    swt_copy.start()
    w_service(2)
    loads[5].wait()
    cot_copy.wait_recv()
    swt_copy.wait_recv()

    for n in range(4):
        cols = slice(n * 256, (n + 1) * 256)
        part = jnp.dot(swt[core].reshape(512, ROWS), cot[:, cols], preferred_element_type=F32)
        part = part + jnp.dot(swt_rx[...].reshape(512, ROWS), cot_sib[:, cols], preferred_element_type=F32)
        tx1[:, :, cols] = part.astype(BF16).reshape(N, 64, 256)

    r1 = {}
    for k in order:
        r1[k] = remote(tx1.at[(a + k) % N, EARLY:64], rx1.at[k - 1], r1_s.at[k - 1], r1_r.at[k - 1], a_peer(k))
        r1[k].start()
    w_service(3)
    ry = {}
    for k in order:
        ry[k] = remote(tx1.at[:, 0:EARLY, shard((y + k) % N)], rxy.at[k - 1], ry_s.at[k - 1], ry_r.at[k - 1],
                       y_peer(k))
        ry[k].start()
    w_service(4)
    own_w.wait()
    for s in range(1, 5):
        owner = (y - s + N) % N
        remote(w_block(owner, other_half), w_block(owner, other_half),
               ws_s.at[s - 1], ws_r.at[s - 1], sibling).wait_recv()
    for s in range(1, 4):
        owner = (y + s) % N
        remote(w_block(owner, other_half), w_block(owner, other_half),
               ws_s.at[4 + s - 1], ws_r.at[4 + s - 1], sibling).wait_recv()

    sum_a[...] = jnp.zeros((ROWS, LANES), F32)
    sum_b[...] = jnp.zeros((ROWS, LANES), F32)
    for n in range(4):
        grad = lax.dot_general(cot[...], w_all[n * 256:(n + 1) * 256, :], (((1,), (1,)), ((), ())),
                               preferred_element_type=F32)
        for i in range(2):
            c = 2 * n + i
            grad_normed = grad[:, i * LANES:(i + 1) * LANES] * dfac[c]
            gwin[c, HALO:HALO + ROWS, :] = grad_normed
            sum_a[...] += grad_normed
            sum_b[...] += grad_normed * normed[c]
    sum_a[...] = jnp.broadcast_to(jnp.sum(sum_a[...], axis=1, keepdims=True) * (1.0 / D), (ROWS, LANES))
    sum_b[...] = jnp.broadcast_to(jnp.sum(sum_b[...], axis=1, keepdims=True) * (1.0 / D), (ROWS, LANES))

    def norm_back(c, carry):
        gwin[c, HALO:HALO + ROWS, :] = inv_b[...] * (
            gwin[c, HALO:HALO + ROWS, :] - sum_a[...] - normed[c] * sum_b[...])
        return carry

    lax.fori_loop(0, N, norm_back, 0)

    ghalo_down = remote(gwin.at[:, ROWS:ROWS + HALO, :], gwin.at[:, 0:HALO, :],
                        ghalo_s.at[0], ghalo_r.at[0], next_dev)
    ghalo_up = remote(gwin.at[:, HALO:2 * HALO, :], gwin.at[:, ROWS + HALO:WIN, :],
                      ghalo_s.at[1], ghalo_r.at[1], prev_dev)
    ghalo_down.start()
    ghalo_up.start()


    def backward_pair(p, first, count, stride):
        def body(group, carry):
            base = pl.multiple_of(first + group * stride, GROUP)
            pair = convolve(gwin, (2 * p, 2 * p + 1), base, True)
            for i in range(2):
                c = 2 * p + i
                fgrad[pl.ds(base, GROUP), c * LANES:(c + 1) * LANES] = pair[i].astype(BF16)
            return carry

        lax.fori_loop(0, count, body, 0)

    late = b >= 2

    def reduce_a():
        for k in range(1, N):
            remote(tx1.at[0, EARLY:64], rx1.at[k - 1], r1_s.at[k - 1], r1_r.at[k - 1], a_peer(N - k)).wait_recv()
        for c in range(N):
            cols = slice(c * LANES, (c + 1) * LANES)
            total = tx1[a, EARLY:64, cols].astype(F32)
            for k in range(1, N):
                total = total + rx1[k - 1, :, cols].astype(F32)
            acc2[2:N, c] = total.reshape(N - 2, 8, LANES)
        for i in range(2, N):
            tx2[i] = acc2[i].reshape(64, LANES).astype(BF16)
        for k in order:
            @pl.when((b + k) % N >= 2)
            def _():
                remote(tx2.at[(b + k) % N], rx2.at[k - 1], r2_s.at[k - 1], r2_r.at[k - 1], b_peer(k)).start()

    def early_y():
        for k in range(1, N):
            remote(rxy.at[k - 1], rxy.at[k - 1], ry_s.at[k - 1], ry_r.at[k - 1], y_peer(N - k)).wait_recv()
        total = tx1[:, 0:EARLY, shard(y)].astype(F32)
        for k in range(1, N):
            total = total + rxy[k - 1].astype(F32)
        txa[...] = total
        for k in order:
            remote(txa.at[(a + k) % N], rxa.at[k - 1], ra_s.at[k - 1], ra_r.at[k - 1], a_peer(k)).start()

    def early_a():
        for k in range(1, N):
            remote(txa.at[0], rxa.at[k - 1], ra_s.at[k - 1], ra_r.at[k - 1], a_peer(N - k)).wait_recv()
        total = txa[a]
        for k in range(1, N):
            total = total + rxa[k - 1]
        txb[...] = total.reshape(2, 8, LANES)
        for k in order:
            @pl.when((b + k) % N < 2)
            def _():
                remote(txb.at[(b + k) % N % 2], rxb.at[k - 1], rb_s.at[k - 1], rb_r.at[k - 1], b_peer(k)).start()

    def reduce_b():
        @pl.when(late)
        def _():
            for k in range(1, N):
                remote(tx2.at[0], rx2.at[k - 1], r2_s.at[k - 1], r2_r.at[k - 1], b_peer(N - k)).wait_recv()
            total = acc2[b].reshape(64, LANES)
            for k in range(1, N):
                total = total + rx2[k - 1].astype(F32)
            tx3[...] = total.reshape(N, 8, LANES)
            for k in order:
                remote(tx3.at[(y + k) % N], rx3.at[k - 1], r3_s.at[k - 1], r3_r.at[k - 1], y_peer(k)).start()

    def finish():
        @pl.when(late)
        def _():
            for k in range(1, N):
                remote(tx3.at[0], rx3.at[k - 1], r3_s.at[k - 1], r3_r.at[k - 1], y_peer(N - k)).wait_recv()
            total = tx3[y]
            for k in range(1, N):
                total = total + rx3[k - 1]
            pgrad[...] = total * (1.0 / 1024)

        @pl.when(jnp.logical_not(late))
        def _():
            for k in range(1, N):
                remote(txb.at[0], rxb.at[k - 1], rb_s.at[k - 1], rb_r.at[k - 1], b_peer(N - k)).wait_recv()
            total = txb[b % 2]
            for k in range(1, N):
                total = total + rxb[k - 1]
            pgrad[...] = total * (1.0 / 1024)

    reduce_a()
    early_y()
    for p in range(4):
        backward_pair(p, GROUP, 2, GROUP)
    ghalo_down.wait_recv()
    ghalo_up.wait_recv()
    backward_pair(0, 0, 2, ROWS - GROUP)
    backward_pair(1, 0, 2, ROWS - GROUP)
    reduce_b()
    early_a()
    backward_pair(2, 0, 2, ROWS - GROUP)
    backward_pair(3, 0, 2, ROWS - GROUP)
    for n in range(4):
        cols = slice(n * 256, (n + 1) * 256)
        out[:, cols] = jnp.dot(swished[...], w_all[:, cols], preferred_element_type=F32).astype(BF16)
    finish()

    for k in range(1, N):
        tap_copies[k].wait_send()
        gain_copies[k].wait_send()
        r1[k].wait_send()
        ry[k].wait_send()
        remote(txa.at[0], rxa.at[k - 1], ra_s.at[k - 1], ra_r.at[k - 1], a_peer(k)).wait_send()

        @pl.when((b + k) % N >= 2)
        def _():
            remote(tx2.at[0], rx2.at[k - 1], r2_s.at[k - 1], r2_r.at[k - 1], b_peer(k)).wait_send()

        @pl.when((b + k) % N < 2)
        def _():
            remote(txb.at[0], rxb.at[k - 1], rb_s.at[k - 1], rb_r.at[k - 1], b_peer(k)).wait_send()

        @pl.when(late)
        def _():
            remote(tx3.at[0], rx3.at[k - 1], r3_s.at[k - 1], r3_r.at[k - 1], y_peer(k)).wait_send()
    for copy in (halo_down, halo_up, ghalo_down, ghalo_up, cot_copy, swt_copy):
        copy.wait_send()
    for copies in (w_right, w_left, w_side):
        for copy in copies.values():
            copy.wait_send()


def deliver(out, fgrad, pgrad, out_to, fgrad_to, pgrad_to, sem):
    copies = [pltpu.make_async_copy(src, dst, sem.at[i]) for i, (src, dst) in enumerate(
        ((out, out_to), (fgrad, fgrad_to), (pgrad, pgrad_to)))]
    for copy in copies:
        copy.start()
    for copy in copies:
        copy.wait()


def per_device(frames, lengths, taps, conv_bias, norm_gain, proj_weight, cotangent):
    dma = pltpu.SemaphoreType.DMA
    vmem = pl.BlockSpec(memory_space=pltpu.VMEM)
    hbm = pl.BlockSpec(memory_space=pltpu.HBM)
    shapes = (
        jax.ShapeDtypeStruct((ROWS, D), BF16),
        jax.ShapeDtypeStruct((ROWS, D), BF16),
        jax.ShapeDtypeStruct((8, LANES), F32),
    )
    scratch = [
        pltpu.VMEM((ROWS, D), BF16), pltpu.VMEM((N, LANES), jnp.int32), pltpu.VMEM((TAPS, LANES), BF16),
        pltpu.VMEM((1, LANES), BF16), pltpu.VMEM((1, LANES), BF16), pltpu.VMEM((ROWS, D), BF16),
        pltpu.VMEM((32, LANES), BF16), pltpu.VMEM((16, LANES), BF16), pltpu.VMEM((32, LANES), F32),
        pltpu.VMEM((N, 32, LANES), BF16), pltpu.VMEM((N, 16, LANES), BF16),
        pltpu.VMEM((N, 32, LANES), F32), pltpu.VMEM((N, 16, LANES), F32),
        pltpu.VMEM((2, HALO, D), BF16),
        pltpu.VMEM((N, WIN, LANES), F32), pltpu.VMEM((N, WIN, LANES), F32),
        pltpu.VMEM((ROWS, LANES), F32), pltpu.VMEM((ROWS, LANES), F32),
        pltpu.VMEM((N, ROWS, LANES), F32), pltpu.VMEM((N, ROWS, LANES), F32),
        pltpu.VMEM((N, ROWS, LANES), F32),
        pltpu.VMEM((ROWS, LANES), F32), pltpu.VMEM((ROWS, LANES), F32), pltpu.VMEM((ROWS, LANES), F32),
        pltpu.VMEM((ROWS, D), BF16),
        pltpu.VMEM((2, N, 64, ROWS), BF16), pltpu.VMEM((N, N, 8, ROWS), F32), pltpu.VMEM((N, 64, ROWS), BF16),
        pltpu.VMEM((ROWS, D), BF16), pltpu.VMEM((D, D), BF16),
        pltpu.VMEM((N, 64, D), BF16), pltpu.VMEM((N - 1, 64 - EARLY, D), BF16),
        pltpu.VMEM((N, N, 8, LANES), F32),
        pltpu.VMEM((N, 64, LANES), BF16), pltpu.VMEM((N - 1, 64, LANES), BF16),
        pltpu.VMEM((N, 8, LANES), F32), pltpu.VMEM((N - 1, 8, LANES), F32),
        pltpu.VMEM((N - 1, N, EARLY, LANES), BF16),
        pltpu.VMEM((N, EARLY, LANES), F32), pltpu.VMEM((N - 1, EARLY, LANES), F32),
        pltpu.VMEM((2, 8, LANES), F32), pltpu.VMEM((N - 1, 8, LANES), F32),
        dma((7,)), dma((7,)), dma((7,)), dma((7,)), dma((2,)), dma((2,)), dma((2,)), dma((2,)),
        dma, dma, dma, dma, dma((4,)), dma((4,)), dma((4,)), dma((4,)), dma((7,)), dma((7,)),
        dma((7,)), dma((7,)), dma((7,)), dma((7,)), dma((7,)), dma((7,)),
        dma((7,)), dma((7,)), dma((7,)), dma((7,)), dma((7,)), dma((7,)), dma((7,)),
    ]
    results = pl.pallas_call(
        fused,
        out_shape=shapes,
        in_specs=[hbm] * 7,
        out_specs=(vmem,) * 3,
        scratch_shapes=scratch,
        compiler_params=pltpu.CompilerParams(
            collective_id=0, has_side_effects=True, vmem_limit_bytes=40 * 1024 * 1024),
        name="fused_module",
    )(*(pltpu.with_memory_space_constraint(value, pltpu.HBM) for value in (
        frames, lengths.reshape(N, LANES), taps, conv_bias.reshape(1, LANES),
        norm_gain.reshape(1, LANES), proj_weight, cotangent)))
    return pl.pallas_call(
        deliver,
        out_shape=shapes,
        in_specs=[vmem] * 3,
        out_specs=(hbm,) * 3,
        scratch_shapes=[dma((3,))],
        name="deliver",
    )(*(pltpu.with_memory_space_constraint(value, pltpu.VMEM) for value in results))


def solution(mesh):
    rows = P(("dp", "fsdp"), None)
    in_specs = (rows, P(), P(None, "fsdp"), P("fsdp"), P("fsdp"), P(None, "fsdp"), rows)
    out_specs = (rows, rows, P("dp", "fsdp"))
    return jax.shard_map(
        per_device, mesh=mesh, in_specs=in_specs, out_specs=out_specs, check_vma=False)
```

```python
import jax
import jax.numpy as jnp
from jax import lax
from jax.experimental import pallas as pl
from jax.experimental.pallas import tpu as pltpu
from jax.sharding import PartitionSpec as P

MESH = pl.DeviceIdType.MESH
F32 = jnp.float32
BF16 = jnp.bfloat16
N = 8
LANES = 128
ROWS = 256
D = 1024
TAPS = 31
HALO = 16
WIN = ROWS + 2 * HALO
GROUP = 64
EARLY = 16


def fused(frames_h, lengths_h, taps_h, bias_h, gain_h, weight, cot_h,
          out, fgrad, pgrad,
          frames, lengths, taps, bias, gain, cot,
          pack, gpack, pack_f, tap_all, gain_all, tap_f, gain_f,
          halo, fwin, gwin, off_b, rem_b,
          conv, normed, dfac, inv_b, sum_a, sum_b,
          swished, swt, swt_f, swt_rx, part_f, cot_sib, w_all,
          tx1, rx1, acc2, tx2, rx2, tx3, rx3, rxy, txa, rxa, txb, rxb,
          tap_s, tap_r, gain_s, gain_r, halo_s, halo_r, ghalo_s, ghalo_r,
          cot_s, cot_r, swt_s, swt_r, wr_s, wr_r, wl_s, wl_r, ws_s, ws_r,
          r1_s, r1_r, r2_s, r2_r, r3_s, r3_r, ry_s, ry_r, ra_s, ra_r, rb_s, rb_r, loc_s):
    dp = lax.axis_index("dp")
    y = lax.axis_index("fsdp")
    core = dp % 2
    z = (dp // 2) % N
    x = dp // (2 * N)
    a = x * (1 - core) + z * core
    b = z * (1 - core) + x * core

    def chip(a_to, b_to):
        return (a_to * (N - (N - 1) * core) + b_to * (1 + (N - 1) * core)) * 2 + core

    def y_peer(k):
        return (dp, (y + k) % N)

    def a_peer(k):
        return (chip((a + k) % N, b), y)

    def b_peer(k):
        return (chip(a, (b + k) % N), y)

    sibling = (dp + 1 - 2 * core, y)
    place = dp * N + y
    count = 128 * N
    after = (place + 1) % count
    before = (place + count - 1) % count
    next_dev = (after // N, after % N)
    prev_dev = (before // N, before % N)

    def remote(src, dst, send, recv, to):
        return pltpu.make_async_remote_copy(
            src_ref=src, dst_ref=dst, send_sem=send, recv_sem=recv,
            device_id=to, device_id_type=MESH)

    loads = [pltpu.make_async_copy(src, dst, loc_s.at[i]) for i, (src, dst) in enumerate((
        (lengths_h, lengths), (taps_h, taps), (bias_h, bias), (gain_h, gain), (frames_h, frames), (cot_h, cot)))]
    for load in loads:
        load.start()

    barrier = pltpu.get_barrier_semaphore()
    order = (4, 3, 5, 2, 6, 1, 7)
    peers = [y_peer(k) for k in order] + [next_dev, prev_dev, sibling]
    for k in order:
        peers += [a_peer(k), b_peer(k)]
    for peer in peers:
        pl.semaphore_signal(barrier, inc=1, device_id=peer, device_id_type=MESH)

    for load in loads[:4]:
        load.wait()

    pack_f[0:TAPS, :] = taps[...].astype(F32)
    pack_f[TAPS:TAPS + 1, :] = bias[...].astype(F32)
    pack[...] = pack_f[...].astype(BF16)
    gpack[...] = jnp.broadcast_to(gain[...].astype(F32), (16, LANES)).astype(BF16)

    pl.semaphore_wait(barrier, len(peers))

    near = (1, 7, 2, 6, 3, 5, 4)
    tap_copies = {}
    gain_copies = {}
    for k in near:
        tap_copies[k] = remote(pack, tap_all.at[y], tap_s.at[k - 1], tap_r.at[k - 1], y_peer(k))
        tap_copies[k].start()
    halo_down = remote(frames_h.at[ROWS - HALO:ROWS], halo.at[0], halo_s.at[0], halo_r.at[0], next_dev)
    halo_up = remote(frames_h.at[0:HALO], halo.at[1], halo_s.at[1], halo_r.at[1], prev_dev)
    halo_down.start()
    halo_up.start()
    half = D // 2
    my_half = pl.ds(pl.multiple_of(core * half, half), half)
    other_half = pl.ds(pl.multiple_of((1 - core) * half, half), half)

    def shard(owner):
        return pl.ds(pl.multiple_of(owner * LANES, LANES), LANES)

    def w_block(owner, rows):
        return w_all.at[rows, shard(owner)]

    right, left = y_peer(1), y_peer(N - 1)
    w_right, w_left, w_side = {}, {}, {}

    quarter = half // 2
    first_part = pl.ds(pl.multiple_of(core * half, quarter), quarter)
    second_part = pl.ds(pl.multiple_of(core * half + quarter, quarter), quarter)

    def send_right(s):
        owner = (y - (s - 1) + N) % N
        rows = first_part if s == 4 else my_half
        src = weight.at[rows, :] if s == 1 else w_block(owner, rows)
        w_right[s] = remote(src, w_block(owner, rows), wr_s.at[s - 1], wr_r.at[s - 1], right)
        w_right[s].start()

    def send_left(s):
        owner = (y + (s - 1)) % N
        rows = second_part if s == 4 else my_half
        src = weight.at[rows, :] if s == 1 else w_block(owner, rows)
        w_left[s] = remote(src, w_block(owner, rows), wl_s.at[s - 1], wl_r.at[s - 1], left)
        w_left[s].start()

    def send_side(slot, owner):
        w_side[slot] = remote(w_block(owner, my_half), w_block(owner, my_half),
                              ws_s.at[slot], ws_r.at[slot], sibling)
        w_side[slot].start()

    def w_service(s):
        below, above = (y - s + N) % N, (y + s) % N
        rows = first_part if s == 4 else my_half
        remote(w_block(below, rows), w_block(below, rows), wr_s.at[s - 1], wr_r.at[s - 1], right).wait_recv()
        if s < 4:
            send_right(s + 1)
            send_side(s - 1, below)
        rows = second_part if s == 4 else my_half
        remote(w_block(above, rows), w_block(above, rows), wl_s.at[s - 1], wl_r.at[s - 1], left).wait_recv()
        if s < 4:
            send_left(s + 1)
            send_side(3 + s, above)
        else:
            send_side(3, below)

    for k in near:
        gain_copies[k] = remote(gpack, gain_all.at[y], gain_s.at[k - 1], gain_r.at[k - 1], y_peer(k))
        gain_copies[k].start()
    send_right(1)
    send_left(1)
    cot_copy = remote(cot_h, cot_sib, cot_s, cot_r, sibling)
    cot_copy.start()
    own_w = pltpu.make_async_copy(weight, w_all.at[:, shard(y)], loc_s.at[6])
    own_w.start()

    ends = lengths[...].astype(F32)
    lane = lax.broadcasted_iota(jnp.int32, (N, LANES), 1)
    row8 = lax.broadcasted_iota(jnp.int32, (N, LANES), 0)
    step = 1
    while step < LANES:
        ends = ends + jnp.where(lane >= step, pltpu.roll(ends, step, 1), 0.0)
        step *= 2
    total = jnp.broadcast_to(jnp.max(ends, axis=1, keepdims=True), (N, LANES))
    before_sum = jnp.where(row8 >= 1, pltpu.roll(total, 1, 0), 0.0)
    step = 1
    while step < N:
        before_sum = before_sum + jnp.where(row8 >= step, pltpu.roll(before_sum, step, 0), 0.0)
        step *= 2
    ends = ends + before_sum - (place * ROWS).astype(F32)
    acc2[0, 0] = ends

    def locate(group, carry):
        base = pl.multiple_of(group * GROUP, GROUP)
        rows = (lax.broadcasted_iota(jnp.int32, (GROUP, LANES), 0) + base).astype(F32)
        start = jnp.full((GROUP, LANES), -1e9, F32)
        stop = jnp.full((GROUP, LANES), 1e9, F32)
        for i in range(N):
            edge = jnp.broadcast_to(acc2[0, 0, i:i + 1, :], (GROUP, LANES))
            passed = edge <= rows
            start = jnp.maximum(start, jnp.where(passed, edge, -1e9))
            stop = jnp.minimum(stop, jnp.where(passed, 1e9, edge))
        first = (-(place * ROWS)).astype(F32)
        start = jnp.maximum(jnp.max(start, axis=1, keepdims=True), first)
        stop = jnp.min(stop, axis=1, keepdims=True)
        off_b[pl.ds(base, GROUP), :] = rows - start
        rem_b[pl.ds(base, GROUP), :] = stop - rows
        return carry

    lax.fori_loop(0, ROWS // GROUP, locate, 0)

    loads[4].wait()
    for c in range(N):
        fwin[c, HALO:HALO + ROWS, :] = frames[:, c * LANES:(c + 1) * LANES].astype(F32)

    def tap_arrives(k):
        source = (y - k + N) % N
        remote(tap_all.at[source], tap_all.at[source], tap_s.at[k - 1], tap_r.at[k - 1],
               y_peer(N - k)).wait_recv()
        tap_f[source] = tap_all[source].astype(F32)
        return source

    def convolve(window, blocks, base, reverse):
        off = off_b[pl.ds(base, GROUP), :]
        rem = rem_b[pl.ds(base, GROUP), :]
        sums = []
        for c in blocks:
            if reverse:
                sums.append(jnp.zeros((GROUP, LANES), F32))
            else:
                sums.append(jnp.broadcast_to(tap_f[c, TAPS:TAPS + 1, :], (GROUP, LANES)))
        for j in range(TAPS):
            d = j - (TAPS - 1) // 2
            together = off >= float(-d) if d < 0 else rem > float(d)
            tap = TAPS - 1 - j if reverse else j
            for i, c in enumerate(blocks):
                value = window[c, pl.ds(base + (j + 1), GROUP), :]
                if d != 0:
                    value = jnp.where(together, value, 0.0)
                sums[i] = sums[i] + tap_f[c, tap:tap + 1, :] * value
        return sums

    def forward_blocks(blocks, first, count, stride):
        def body(group, carry):
            base = pl.multiple_of(first + group * stride, GROUP)
            for c, value in zip(blocks, convolve(fwin, blocks, base, False)):
                conv[c, pl.ds(base, GROUP), :] = value
            return carry

        lax.fori_loop(0, count, body, 0)

    tap_f[y] = pack[...].astype(F32)
    forward_blocks((y,), GROUP, 2, GROUP)
    blocks = (tap_arrives(1), tap_arrives(7))
    forward_blocks(blocks, GROUP, 2, GROUP)
    halo_down.wait_recv()
    halo_up.wait_recv()
    for c in range(N):
        fwin[c, 0:HALO, :] = halo[0, :, c * LANES:(c + 1) * LANES].astype(F32)
        fwin[c, HALO + ROWS:WIN, :] = halo[1, :, c * LANES:(c + 1) * LANES].astype(F32)
    forward_blocks(blocks, 0, 2, ROWS - GROUP)
    forward_blocks((tap_arrives(2), tap_arrives(6)), 0, 4, GROUP)
    w_service(1)
    forward_blocks((tap_arrives(3), tap_arrives(5)), 0, 4, GROUP)
    last = tap_arrives(4)
    forward_blocks((y, last), 0, 2, ROWS - GROUP)
    forward_blocks((last,), GROUP, 2, GROUP)

    def over_features(make):
        def body(group, carry):
            base = pl.multiple_of(group * GROUP, GROUP)
            rows = pl.ds(base, GROUP)
            sum_a[rows, :] = make(rows)
            return carry

        lax.fori_loop(0, ROWS // GROUP, body, 0)
        return jnp.sum(sum_a[...], axis=1, keepdims=True) * (1.0 / D)

    def plain(rows):
        total = conv[0, rows, :]
        for c in range(1, N):
            total = total + conv[c, rows, :]
        return total

    sum_b[...] = jnp.broadcast_to(over_features(plain), (ROWS, LANES))

    def squares(rows):
        mean = sum_b[rows, :]
        total = jnp.zeros((GROUP, LANES), F32)
        for c in range(N):
            centre = conv[c, rows, :] - mean
            total = total + centre * centre
        return total

    inv_b[...] = jnp.broadcast_to(lax.rsqrt(over_features(squares) + 1e-05), (ROWS, LANES))

    gain_f[y] = gpack[...].astype(F32)
    for k in range(1, N):
        source = (y - k + N) % N
        remote(gain_all.at[source], gain_all.at[source], gain_s.at[k - 1], gain_r.at[k - 1],
               y_peer(N - k)).wait_recv()
        gain_f[source] = gain_all[source].astype(F32)

    def swish_block(c, carry):
        gain_row = gain_f[c, 0:1, :]
        for h in range(2):
            rows = pl.ds(h * 128, 128)
            unit = (conv[c, rows, :] - sum_b[rows, :]) * inv_b[rows, :]
            normed[c, rows, :] = unit
            scaled = unit * gain_row
            gate = 1.0 / (1.0 + jnp.exp(-scaled))
            sw = (scaled * gate).astype(BF16)
            dfac[c, rows, :] = (gate + scaled * gate * (1.0 - gate)) * gain_row
            swished[rows, shard(c)] = sw
            turned = jnp.transpose(sw.astype(F32)).reshape(N, 2, 8, 128)
            swt[0, c, :, h * 128:(h + 1) * 128] = turned[:, 0].reshape(64, 128).astype(BF16)
            swt_f[:, c, :, h * 128:(h + 1) * 128] = turned[:, 1]
        return carry

    lax.fori_loop(0, N, swish_block, 0)
    for i in range(N):
        swt[1, i] = swt_f[i].reshape(64, ROWS).astype(BF16)

    swt_copy = remote(swt.at[1 - core], swt_rx, swt_s, swt_r, sibling)
    swt_copy.start()
    loads[5].wait()
    for n in range(4):
        cols = slice(n * 256, (n + 1) * 256)
        part_f[:, cols] = jnp.dot(swt[core].reshape(512, ROWS), cot[:, cols], preferred_element_type=F32)
    w_service(2)
    cot_copy.wait_recv()
    swt_copy.wait_recv()

    for n in range(4):
        cols = slice(n * 256, (n + 1) * 256)
        part = part_f[:, cols]
        part = part + jnp.dot(swt_rx[...].reshape(512, ROWS), cot_sib[:, cols], preferred_element_type=F32)
        tx1[:, :, cols] = part.astype(BF16).reshape(N, 64, 256)

    r1 = {}
    for k in order:
        r1[k] = remote(tx1.at[(a + k) % N, EARLY:64], rx1.at[k - 1], r1_s.at[k - 1], r1_r.at[k - 1], a_peer(k))
        r1[k].start()
    w_service(3)
    ry = {}
    for k in order:
        ry[k] = remote(tx1.at[:, 0:EARLY, shard((y + k) % N)], rxy.at[k - 1], ry_s.at[k - 1], ry_r.at[k - 1],
                       y_peer(k))
        ry[k].start()
    w_service(4)
    own_w.wait()
    for s in range(1, 5):
        owner = (y - s + N) % N
        remote(w_block(owner, other_half), w_block(owner, other_half),
               ws_s.at[s - 1], ws_r.at[s - 1], sibling).wait_recv()
    for s in range(1, 4):
        owner = (y + s) % N
        remote(w_block(owner, other_half), w_block(owner, other_half),
               ws_s.at[4 + s - 1], ws_r.at[4 + s - 1], sibling).wait_recv()

    sum_a[...] = jnp.zeros((ROWS, LANES), F32)
    sum_b[...] = jnp.zeros((ROWS, LANES), F32)
    for n in range(4):
        grad = lax.dot_general(cot[...], w_all[n * 256:(n + 1) * 256, :], (((1,), (1,)), ((), ())),
                               preferred_element_type=F32)
        for i in range(2):
            c = 2 * n + i
            grad_normed = grad[:, i * LANES:(i + 1) * LANES] * dfac[c]
            gwin[c, HALO:HALO + ROWS, :] = grad_normed
            sum_a[...] += grad_normed
            sum_b[...] += grad_normed * normed[c]
    sum_a[...] = jnp.broadcast_to(jnp.sum(sum_a[...], axis=1, keepdims=True) * (1.0 / D), (ROWS, LANES))
    sum_b[...] = jnp.broadcast_to(jnp.sum(sum_b[...], axis=1, keepdims=True) * (1.0 / D), (ROWS, LANES))

    def norm_back(c, carry):
        gwin[c, HALO:HALO + ROWS, :] = inv_b[...] * (
            gwin[c, HALO:HALO + ROWS, :] - sum_a[...] - normed[c] * sum_b[...])
        return carry

    lax.fori_loop(0, N, norm_back, 0)

    ghalo_down = remote(gwin.at[:, ROWS:ROWS + HALO, :], gwin.at[:, 0:HALO, :],
                        ghalo_s.at[0], ghalo_r.at[0], next_dev)
    ghalo_up = remote(gwin.at[:, HALO:2 * HALO, :], gwin.at[:, ROWS + HALO:WIN, :],
                      ghalo_s.at[1], ghalo_r.at[1], prev_dev)
    ghalo_down.start()
    ghalo_up.start()


    def backward_pair(p, first, count, stride):
        def body(group, carry):
            base = pl.multiple_of(first + group * stride, GROUP)
            pair = convolve(gwin, (2 * p, 2 * p + 1), base, True)
            for i in range(2):
                c = 2 * p + i
                fgrad[pl.ds(base, GROUP), c * LANES:(c + 1) * LANES] = pair[i].astype(BF16)
            return carry

        lax.fori_loop(0, count, body, 0)

    late = b >= 2

    def reduce_a():
        for k in range(1, N):
            remote(tx1.at[0, EARLY:64], rx1.at[k - 1], r1_s.at[k - 1], r1_r.at[k - 1], a_peer(N - k)).wait_recv()
        for c in range(N):
            cols = slice(c * LANES, (c + 1) * LANES)
            total = tx1[a, EARLY:64, cols].astype(F32)
            for k in range(1, N):
                total = total + rx1[k - 1, :, cols].astype(F32)
            acc2[2:N, c] = total.reshape(N - 2, 8, LANES)
        for i in range(2, N):
            tx2[i] = acc2[i].reshape(64, LANES).astype(BF16)
        for k in order:
            @pl.when((b + k) % N >= 2)
            def _():
                remote(tx2.at[(b + k) % N], rx2.at[k - 1], r2_s.at[k - 1], r2_r.at[k - 1], b_peer(k)).start()

    def early_y():
        for k in range(1, N):
            remote(rxy.at[k - 1], rxy.at[k - 1], ry_s.at[k - 1], ry_r.at[k - 1], y_peer(N - k)).wait_recv()
        total = tx1[:, 0:EARLY, shard(y)].astype(F32)
        for k in range(1, N):
            total = total + rxy[k - 1].astype(F32)
        txa[...] = total
        for k in order:
            remote(txa.at[(a + k) % N], rxa.at[k - 1], ra_s.at[k - 1], ra_r.at[k - 1], a_peer(k)).start()

    def early_a():
        for k in range(1, N):
            remote(txa.at[0], rxa.at[k - 1], ra_s.at[k - 1], ra_r.at[k - 1], a_peer(N - k)).wait_recv()
        total = txa[a]
        for k in range(1, N):
            total = total + rxa[k - 1]
        txb[...] = total.reshape(2, 8, LANES)
        for k in order:
            @pl.when((b + k) % N < 2)
            def _():
                remote(txb.at[(b + k) % N % 2], rxb.at[k - 1], rb_s.at[k - 1], rb_r.at[k - 1], b_peer(k)).start()

    def reduce_b():
        @pl.when(late)
        def _():
            for k in range(1, N):
                remote(tx2.at[0], rx2.at[k - 1], r2_s.at[k - 1], r2_r.at[k - 1], b_peer(N - k)).wait_recv()
            total = acc2[b].reshape(64, LANES)
            for k in range(1, N):
                total = total + rx2[k - 1].astype(F32)
            tx3[...] = total.reshape(N, 8, LANES)
            for k in order:
                remote(tx3.at[(y + k) % N], rx3.at[k - 1], r3_s.at[k - 1], r3_r.at[k - 1], y_peer(k)).start()

    def finish():
        @pl.when(late)
        def _():
            for k in range(1, N):
                remote(tx3.at[0], rx3.at[k - 1], r3_s.at[k - 1], r3_r.at[k - 1], y_peer(N - k)).wait_recv()
            total = tx3[y]
            for k in range(1, N):
                total = total + rx3[k - 1]
            pgrad[...] = total * (1.0 / 1024)

        @pl.when(jnp.logical_not(late))
        def _():
            for k in range(1, N):
                remote(txb.at[0], rxb.at[k - 1], rb_s.at[k - 1], rb_r.at[k - 1], b_peer(N - k)).wait_recv()
            total = txb[b % 2]
            for k in range(1, N):
                total = total + rxb[k - 1]
            pgrad[...] = total * (1.0 / 1024)

    reduce_a()
    early_y()
    for p in range(4):
        backward_pair(p, GROUP, 2, GROUP)
    ghalo_down.wait_recv()
    ghalo_up.wait_recv()
    backward_pair(0, 0, 2, ROWS - GROUP)
    backward_pair(1, 0, 2, ROWS - GROUP)
    reduce_b()
    early_a()
    backward_pair(2, 0, 2, ROWS - GROUP)
    backward_pair(3, 0, 2, ROWS - GROUP)
    for n in range(4):
        cols = slice(n * 256, (n + 1) * 256)
        out[:, cols] = jnp.dot(swished[...], w_all[:, cols], preferred_element_type=F32).astype(BF16)
    finish()

    for k in range(1, N):
        tap_copies[k].wait_send()
        gain_copies[k].wait_send()
        r1[k].wait_send()
        ry[k].wait_send()
        remote(txa.at[0], rxa.at[k - 1], ra_s.at[k - 1], ra_r.at[k - 1], a_peer(k)).wait_send()

        @pl.when((b + k) % N >= 2)
        def _():
            remote(tx2.at[0], rx2.at[k - 1], r2_s.at[k - 1], r2_r.at[k - 1], b_peer(k)).wait_send()

        @pl.when((b + k) % N < 2)
        def _():
            remote(txb.at[0], rxb.at[k - 1], rb_s.at[k - 1], rb_r.at[k - 1], b_peer(k)).wait_send()

        @pl.when(late)
        def _():
            remote(tx3.at[0], rx3.at[k - 1], r3_s.at[k - 1], r3_r.at[k - 1], y_peer(k)).wait_send()
    for copy in (halo_down, halo_up, ghalo_down, ghalo_up, cot_copy, swt_copy):
        copy.wait_send()
    for copies in (w_right, w_left, w_side):
        for copy in copies.values():
            copy.wait_send()


def deliver(out, fgrad, pgrad, out_to, fgrad_to, pgrad_to, sem):
    copies = [pltpu.make_async_copy(src, dst, sem.at[i]) for i, (src, dst) in enumerate(
        ((out, out_to), (fgrad, fgrad_to), (pgrad, pgrad_to)))]
    for copy in copies:
        copy.start()
    for copy in copies:
        copy.wait()


def per_device(frames, lengths, taps, conv_bias, norm_gain, proj_weight, cotangent):
    dma = pltpu.SemaphoreType.DMA
    vmem = pl.BlockSpec(memory_space=pltpu.VMEM)
    hbm = pl.BlockSpec(memory_space=pltpu.HBM)
    shapes = (
        jax.ShapeDtypeStruct((ROWS, D), BF16),
        jax.ShapeDtypeStruct((ROWS, D), BF16),
        jax.ShapeDtypeStruct((8, LANES), F32),
    )
    scratch = [
        pltpu.VMEM((ROWS, D), BF16), pltpu.VMEM((N, LANES), jnp.int32), pltpu.VMEM((TAPS, LANES), BF16),
        pltpu.VMEM((1, LANES), BF16), pltpu.VMEM((1, LANES), BF16), pltpu.VMEM((ROWS, D), BF16),
        pltpu.VMEM((32, LANES), BF16), pltpu.VMEM((16, LANES), BF16), pltpu.VMEM((32, LANES), F32),
        pltpu.VMEM((N, 32, LANES), BF16), pltpu.VMEM((N, 16, LANES), BF16),
        pltpu.VMEM((N, 32, LANES), F32), pltpu.VMEM((N, 16, LANES), F32),
        pltpu.VMEM((2, HALO, D), BF16),
        pltpu.VMEM((N, WIN, LANES), F32), pltpu.VMEM((N, WIN, LANES), F32),
        pltpu.VMEM((ROWS, LANES), F32), pltpu.VMEM((ROWS, LANES), F32),
        pltpu.VMEM((N, ROWS, LANES), F32), pltpu.VMEM((N, ROWS, LANES), F32),
        pltpu.VMEM((N, ROWS, LANES), F32),
        pltpu.VMEM((ROWS, LANES), F32), pltpu.VMEM((ROWS, LANES), F32), pltpu.VMEM((ROWS, LANES), F32),
        pltpu.VMEM((ROWS, D), BF16),
        pltpu.VMEM((2, N, 64, ROWS), BF16), pltpu.VMEM((N, N, 8, ROWS), F32), pltpu.VMEM((N, 64, ROWS), BF16), pltpu.VMEM((512, D), F32),
        pltpu.VMEM((ROWS, D), BF16), pltpu.VMEM((D, D), BF16),
        pltpu.VMEM((N, 64, D), BF16), pltpu.VMEM((N - 1, 64 - EARLY, D), BF16),
        pltpu.VMEM((N, N, 8, LANES), F32),
        pltpu.VMEM((N, 64, LANES), BF16), pltpu.VMEM((N - 1, 64, LANES), BF16),
        pltpu.VMEM((N, 8, LANES), F32), pltpu.VMEM((N - 1, 8, LANES), F32),
        pltpu.VMEM((N - 1, N, EARLY, LANES), BF16),
        pltpu.VMEM((N, EARLY, LANES), F32), pltpu.VMEM((N - 1, EARLY, LANES), F32),
        pltpu.VMEM((2, 8, LANES), F32), pltpu.VMEM((N - 1, 8, LANES), F32),
        dma((7,)), dma((7,)), dma((7,)), dma((7,)), dma((2,)), dma((2,)), dma((2,)), dma((2,)),
        dma, dma, dma, dma, dma((4,)), dma((4,)), dma((4,)), dma((4,)), dma((7,)), dma((7,)),
        dma((7,)), dma((7,)), dma((7,)), dma((7,)), dma((7,)), dma((7,)),
        dma((7,)), dma((7,)), dma((7,)), dma((7,)), dma((7,)), dma((7,)), dma((7,)),
    ]
    results = pl.pallas_call(
        fused,
        out_shape=shapes,
        in_specs=[hbm] * 7,
        out_specs=(vmem,) * 3,
        scratch_shapes=scratch,
        compiler_params=pltpu.CompilerParams(
            collective_id=0, has_side_effects=True, vmem_limit_bytes=40 * 1024 * 1024),
        name="fused_module",
    )(*(pltpu.with_memory_space_constraint(value, pltpu.HBM) for value in (
        frames, lengths.reshape(N, LANES), taps, conv_bias.reshape(1, LANES),
        norm_gain.reshape(1, LANES), proj_weight, cotangent)))
    return pl.pallas_call(
        deliver,
        out_shape=shapes,
        in_specs=[vmem] * 3,
        out_specs=(hbm,) * 3,
        scratch_shapes=[dma((3,))],
        name="deliver",
    )(*(pltpu.with_memory_space_constraint(value, pltpu.VMEM) for value in results))


def solution(mesh):
    rows = P(("dp", "fsdp"), None)
    in_specs = (rows, P(), P(None, "fsdp"), P("fsdp"), P("fsdp"), P(None, "fsdp"), rows)
    out_specs = (rows, rows, P("dp", "fsdp"))
    return jax.shard_map(
        per_device, mesh=mesh, in_specs=in_specs, out_specs=out_specs, check_vma=False)
```
